128 devices in a mesh: ctx: 16 (over z, y), ep: 8 (over x, core).
Axes of the slice: x: 4, y: 4, z: 4, core: 2. Of those that a mesh axis runs over, the one named last changes fastest.
Arguments:
- queries: bfloat16 [256, 2, 128, 576], P('ep'), may hold values from -440 to 440
- prompt_latent: bfloat16 [32768, 576], P('ctx'), may hold values from -6.1 to 6.1
- new_latent: bfloat16 [256, 2, 576], P('ep'), may hold values from -6 to 6
- blocks: int32 [256, 32], P('ep'), may hold values from 0 to 511, as said below
- value_up: bfloat16 [128, 512, 128], P(('ctx', 'ep')), may hold values from -0.75 to 0.75
- w_out: bfloat16 [16384, 7168], P(('ctx', 'ep')), may hold values from -0.1875 to 0.1875
- residual: bfloat16 [512, 7168], P(('ctx', 'ep')), may hold values from -1.5 to 1.5
- norm_gain: float32 [7168], replicated, may hold values from 0.1 to 1.9
- router: bfloat16 [7168, 16], replicated, may hold values from -0.0625 to 0.0625
- routes: int32 [512, 8], P(('ctx', 'ep')), may hold values from 0 to 15, as said below
- bucket_slots: int32 [512, 8], P(('ctx', 'ep')), may hold values from 0 to 3, as said below
- w_gate: bfloat16 [16, 7168, 2048], P('ctx', None, 'ep'), may hold values from -0.0625 to 0.0625
- w_up: bfloat16 [16, 7168, 2048], P('ctx', None, 'ep'), may hold values from -0.0625 to 0.0625
- w_down: bfloat16 [16, 2048, 7168], P('ctx', 'ep'), may hold values from -0.25 to 0.25
Outputs:
- layer_out: bfloat16 [512, 7168], P(('ctx', 'ep'))
The draws below stay inside these ranges and needn't reach their ends.
Inputs may be any that keep to these rules, and one draw needn't show every extreme that they name: A sample's 32 blocks are distinct. Counting blocks by shard (the 32 consecutive blocks of one index of ctx), each sample has exactly 8 in one shard drawn from the seed, and its other 24 blocks are spread over the other shards as evenly as possible. `routes`: each row names 8 distinct experts; in each aligned block of 4 rows (the rows of one device) some expert is named by every row. `bucket_slots`: within the 4 rows of one device, the rows naming one expert hold the slots 0, 1, 2 and so on for that expert, in an order of the rows drawn from the seed and common to all experts of that device.
All inputs are finite; a program needn't handle non-finite values.
Results may differ from the reference program's by a relative error of at most 0.023.
Values may be sent and summed in bfloat16 or wider, within the bound.
No kernel may reach another device: no remote copies, remote signals or barrier semaphores. Data moves between devices by JAX's collectives and lax.ppermute only.
A program may use at most 192 MiB of HBM per device.

```python
import jax
import jax.numpy as jnp
from jax import lax

D = 7168
FF = 2048
HEADS = 128
KV_RANK = 512
ROPE = 64
VDIM = 128
TOP_K = 8
EXPERTS = 16
BLOCK = 64
SEL = 32
CAPB = 8
CAP = 2
STEPS = 2
SAMPLES = 256
PROMPT = 32768
BLK_DEV = 32
TOKENS = 512
TOK_DEV = 4
N_CTX = 16
N_EP = 8


def base_prompt(key):
    key = jax.random.fold_in(key, 11)
    first_key = jax.random.fold_in(key, 0)
    values = jax.random.normal(first_key, (PROMPT, KV_RANK + ROPE), jnp.float32)
    return jnp.clip(values, -6.0, 6.0)


def pick_blocks(key):
    key = jax.random.fold_in(key, 12)
    hot_key, shard_key, offset_key, shuffle_key = jax.random.split(key, 4)
    hot_shard = jax.random.randint(hot_key, (SAMPLES,), 0, N_CTX)
    shard_perm = jax.vmap(lambda one_key: jax.random.permutation(one_key, N_CTX - 1))(jax.random.split(shard_key, SAMPLES))
    offset_perm = jax.vmap(lambda one_key: jax.random.permutation(one_key, BLK_DEV))(jax.random.split(offset_key, SAMPLES))
    shuffle = jax.vmap(lambda one_key: jax.random.permutation(one_key, SEL))(jax.random.split(shuffle_key, SAMPLES))
    listing = jnp.arange(SEL)
    remainder = jnp.maximum(listing - CAPB, 0)
    other_shard = (hot_shard[:, None] + 1 + shard_perm[:, remainder % (N_CTX - 1)]) % N_CTX
    shard_of = jnp.where(listing[None, :] < CAPB, hot_shard[:, None], other_shard)
    position = jnp.where(listing < CAPB, listing, CAPB + remainder // (N_CTX - 1))
    offset = offset_perm[:, position]
    listed = shard_of * BLK_DEV + offset
    return jnp.take_along_axis(listed, shuffle, axis=1).astype(jnp.int32)


def shared_rope(key):
    key = jax.random.fold_in(key, 13)
    return jnp.clip(jax.random.normal(key, (SAMPLES, ROPE), jnp.float32), -3.0, 3.0)


def routing(key):
    key = jax.random.fold_in(key, 14)
    hot_key, pick_key, place_key, rank_key = jax.random.split(key, 4)
    groups = TOKENS // TOK_DEV
    hot_expert = jax.random.randint(hot_key, (groups,), 0, EXPERTS)
    owners = jnp.repeat(hot_expert, TOK_DEV)
    others = jax.vmap(lambda one_key: jax.random.permutation(one_key, EXPERTS - 1))(jax.random.split(pick_key, TOKENS))[:, :TOP_K - 1]
    chosen = jnp.concatenate([owners[:, None], (owners[:, None] + 1 + others) % EXPERTS], axis=1)
    placing = jax.vmap(lambda one_key: jax.random.permutation(one_key, TOP_K))(jax.random.split(place_key, TOKENS))
    routes = jnp.take_along_axis(chosen, placing, axis=1).astype(jnp.int32)
    priority = jax.vmap(lambda one_key: jax.random.permutation(one_key, TOK_DEV))(jax.random.split(rank_key, groups))
    member = jnp.any(routes[:, :, None] == jnp.arange(EXPERTS)[None, None, :], axis=1).astype(jnp.int32)
    member = member.reshape(groups, TOK_DEV, EXPERTS)
    earlier = (priority[:, None, :] < priority[:, :, None]).astype(jnp.int32)
    before = jnp.einsum('gab,gbe->gae', earlier, member).reshape(TOKENS, EXPERTS)
    bucket_slots = jnp.take_along_axis(before, routes, axis=1).astype(jnp.int32)
    return (routes, bucket_slots)


def draw_blocks(key, part):
    return pick_blocks(key)


def draw_routes(key, part):
    routes, bucket_slots = routing(key)
    return routes


def draw_bucket_slots(key, part):
    routes, bucket_slots = routing(key)
    return bucket_slots


def draw_prompt_latent(key, part):
    prompt = base_prompt(key)
    return prompt.astype(jnp.bfloat16)


def draw_new_latent(key, part):
    common = shared_rope(key)
    key = jax.random.fold_in(key, 2)
    values = jnp.clip(jax.random.normal(key, (SAMPLES, STEPS, KV_RANK + ROPE), jnp.float32), -6.0, 6.0)
    rope_part = jnp.clip(common[:, None, :] + 0.5 * values[..., KV_RANK:], -6.0, 6.0)
    return jnp.concatenate([values[..., :KV_RANK], rope_part], axis=-1).astype(jnp.bfloat16)


def draw_queries(key, part):
    common = shared_rope(key)
    key = jax.random.fold_in(key, 1)
    noise_key = jax.random.fold_in(key, 0)
    values = jnp.clip(jax.random.normal(noise_key, (SAMPLES, STEPS, HEADS, KV_RANK + ROPE), jnp.float32), -6.0, 6.0)
    values = jnp.concatenate([values[..., :KV_RANK], values[..., KV_RANK:] + 1.5 * common[:, None, None, :]], axis=-1)
    return values.astype(jnp.bfloat16)


def levels(rng, extent, cuts, least, largest):
    loudness, own = 1.0, jax.random.fold_in(rng, 6)
    for dim, parts in cuts:
        draws = jnp.exp(jax.random.uniform(jax.random.fold_in(own, dim), (parts,), jnp.float32, least / len(cuts), largest / len(cuts)))
        loudness = loudness * jnp.repeat(draws, extent[dim] // parts).reshape([-1 if axis == dim else 1 for axis in range(len(extent))])
    return loudness


def normal_values(own_key, dims, scale, bound, pieces=(), held_as=jnp.bfloat16):
    result = jax.random.normal(own_key, dims, jnp.float32) * scale
    if len(pieces) > 0:
        result = levels(own_key, dims, pieces, -0.22, 0.18) * result
    return jnp.clip(result, min=-bound, max=bound).astype(held_as)


def setup_inputs(seed: int = 0) -> dict:
    keys = jax.random.split(jax.random.key(seed), 15)
    return {
        "queries": draw_queries(jax.random.fold_in(keys[14], 71), 0),
        "prompt_latent": draw_prompt_latent(jax.random.fold_in(keys[14], 71), 0),
        "new_latent": draw_new_latent(jax.random.fold_in(keys[14], 71), 0),
        "blocks": draw_blocks(jax.random.fold_in(keys[14], 71), 0),
        "value_up": normal_values(keys[4], (HEADS, KV_RANK, VDIM), (KV_RANK // 8) ** -0.5, 0.75, ((0, 128),)),
        "w_out": normal_values(keys[5], (HEADS * VDIM, D), (HEADS * VDIM // 16) ** -0.5, 0.1875, ((0, 128),)),
        "residual": normal_values(keys[6], (TOKENS, D), 0.25, 1.5, ((0, 128),)),
        "norm_gain": jnp.clip(1.0 + 0.18 * jax.random.normal(keys[7], (D,), jnp.float32), 0.1, 1.9),
        "router": normal_values(keys[8], (D, EXPERTS), D ** -0.5, 0.0625),
        "routes": draw_routes(jax.random.fold_in(keys[14], 71), 0),
        "bucket_slots": draw_bucket_slots(jax.random.fold_in(keys[14], 71), 0),
        "w_gate": normal_values(keys[11], (EXPERTS, D, FF), D ** -0.5, 0.0625, ((0, 16), (2, 8))),
        "w_up": normal_values(keys[12], (EXPERTS, D, FF), D ** -0.5, 0.0625, ((0, 16), (2, 8))),
        "w_down": normal_values(keys[13], (EXPERTS, FF, D), (FF // 4) ** -0.5, 0.25, ((0, 16), (1, 8))),
    }


score_scale = 192.0 ** (-0.5)

def attend_sample(inputs, prompt_latent):
    query_rows, own_keys, listed = inputs
    offsets = jnp.arange(BLOCK, dtype=jnp.int32)
    key_rows = (listed.astype(jnp.int32)[:, None] * BLOCK + offsets[None, :]).reshape(-1).astype(jnp.int32)
    gathered = jnp.take(prompt_latent, key_rows, axis=0)
    every_key = jnp.concatenate([gathered, own_keys], axis=0)
    flat_query = query_rows.reshape(STEPS * HEADS, KV_RANK + ROPE)
    scores = jnp.dot(flat_query, every_key.T, preferred_element_type=jnp.float32) * score_scale
    query_step = jnp.arange(STEPS * HEADS, dtype=jnp.int32) // HEADS
    key_step = jnp.arange(SEL * BLOCK + STEPS, dtype=jnp.int32) - SEL * BLOCK
    allowed = key_step[None, :] <= query_step[:, None]
    scores = jnp.where(allowed, scores, -jnp.inf)
    row_max = lax.optimization_barrier(jnp.max(scores, axis=1, keepdims=True))
    weights = jnp.exp(scores - row_max)
    row_total = lax.optimization_barrier(jnp.sum(weights, axis=1, keepdims=True))
    mixed_latent = jnp.dot(weights.astype(jnp.bfloat16), every_key[:, :KV_RANK], preferred_element_type=jnp.float32)
    return (mixed_latent / row_total).astype(jnp.bfloat16).reshape(STEPS, HEADS, KV_RANK)

def expert_output(index, normed, w_gate, w_up, w_down):
    gate_act = jnp.dot(normed, w_gate[index], preferred_element_type=jnp.float32)
    up_act = jnp.dot(normed, w_up[index], preferred_element_type=jnp.float32)
    inner_act = (jax.nn.silu(gate_act) * up_act).astype(jnp.bfloat16)
    group_width = FF // N_EP
    grouped = jnp.einsum('tgf,gfd->tgd', inner_act.reshape(TOKENS, N_EP, group_width).astype(jnp.float32), w_down[index].reshape(N_EP, group_width, D).astype(jnp.float32))
    rounded = lax.optimization_barrier(grouped.astype(jnp.bfloat16))
    return lax.optimization_barrier(jnp.sum(rounded.astype(jnp.float32), axis=1))

def reference(queries, prompt_latent, new_latent, blocks, value_up, w_out, residual, norm_gain, router, routes, bucket_slots, w_gate, w_up, w_down):
    latent_out = lax.map(lambda inputs: attend_sample(inputs, prompt_latent), (queries, new_latent, blocks))
    head_values = jnp.einsum('sthr,hrv->sthv', latent_out.astype(jnp.float32), value_up.astype(jnp.float32)).astype(jnp.bfloat16)
    head_flat = head_values.reshape(SAMPLES * STEPS, HEADS * VDIM)
    attention = jnp.dot(head_flat, w_out, preferred_element_type=jnp.float32)
    hidden_state = (residual.astype(jnp.float32) + attention).astype(jnp.bfloat16)
    hidden_wide = hidden_state.astype(jnp.float32)
    mean_square = lax.optimization_barrier(jnp.mean(hidden_wide * hidden_wide, axis=1, keepdims=True))
    normed = (hidden_wide * lax.rsqrt(mean_square + 1e-06) * norm_gain).astype(jnp.bfloat16)
    affinity = jax.nn.sigmoid(jnp.dot(normed, router, preferred_element_type=jnp.float32))
    picked_aff = jnp.take_along_axis(affinity, routes, axis=1)
    combine_w = 2.5 * picked_aff / lax.optimization_barrier(jnp.sum(picked_aff, axis=1, keepdims=True))
    route_weight = jnp.where(bucket_slots < CAP, combine_w, jnp.zeros_like(combine_w))
    expert_ids = jnp.arange(EXPERTS, dtype=jnp.int32)
    weight_table = lax.optimization_barrier(jnp.sum(route_weight[:, :, None] * (routes[:, :, None] == expert_ids[None, None, :]).astype(route_weight.dtype), axis=1))

    def accumulate(carry, index):
        produced = expert_output(index, normed, w_gate, w_up, w_down)
        column = lax.dynamic_slice_in_dim(weight_table, index, 1, 1)
        return (carry + column * produced, None)
    moe_sum, unused = lax.scan(accumulate, jnp.zeros((TOKENS, D), hidden_wide.dtype), expert_ids)
    return (hidden_wide + moe_sum).astype(jnp.bfloat16)
```

```python
import jax
import jax.numpy as jnp
from jax import lax
from jax.experimental import pallas as pl
from jax.experimental.pallas import tpu as pltpu
from jax.sharding import PartitionSpec as P

BLOCK = 64
CAPB = 8
CAP = 2
PAIR = 2 * BLOCK
OWN_ROWS = 16

score_scale = 192.0 ** (-0.5)
masked_score = -1e30
BF = jnp.bfloat16
F32 = jnp.float32


def attend_kernel(
    count_ref, table_ref, own_ref, q_ref, prompt_ref, new_ref, acc_ref, stat_ref, keys, acc, top, tot
):
    sample = pl.program_id(0)
    rows = q_ref.shape[1]
    rank = acc_ref.shape[2]
    count = count_ref[sample]
    own = own_ref[0]
    chunks = (count + own + 1) // 2

    @pl.when(sample == 0)
    def _():
        keys[...] = jnp.zeros_like(keys)

    top[...] = jnp.full(top.shape, masked_score, F32)
    tot[...] = jnp.zeros_like(tot)
    acc[...] = jnp.zeros_like(acc)
    column = lax.broadcasted_iota(jnp.int32, (rows, PAIR), 1)
    step = lax.broadcasted_iota(jnp.int32, (rows, PAIR), 0) // (rows // 2)

    def body(chunk, carry):
        for half in range(2):
            place = 2 * chunk + half

            @pl.when(place < count)
            def _():
                start = pl.multiple_of(table_ref[sample, jnp.minimum(place, CAPB - 1)] * BLOCK, BLOCK)
                keys[half * BLOCK : (half + 1) * BLOCK, :] = prompt_ref[pl.ds(start, BLOCK), :]

            @pl.when((place == count) & (own == 1))
            def _():
                keys[half * BLOCK : half * BLOCK + OWN_ROWS, :] = new_ref[0]

        place = 2 * chunk + column // BLOCK
        within = column % BLOCK
        live = (place < count) | ((place == count) & (own == 1) & (within <= step))
        scores = (
            lax.dot_general(
                q_ref[0], keys[...], (((1,), (1,)), ((), ())), preferred_element_type=F32
            )
            * score_scale
        )
        scores = jnp.where(live, scores, masked_score)
        old_top = top[...]
        new_top = jnp.maximum(old_top, jnp.max(scores, axis=1, keepdims=True))
        factor = jnp.exp(old_top - new_top)
        weight = jnp.where(live, jnp.exp(scores - new_top[:, :1]), 0.0)
        top[...] = new_top
        tot[...] = tot[...] * factor + jnp.sum(weight, axis=1, keepdims=True)
        acc[...] = acc[...] * factor[:, :1] + jnp.dot(
            weight.astype(BF), keys[:, :rank], preferred_element_type=F32
        )
        return carry

    lax.fori_loop(0, chunks, body, 0)
    acc_ref[0] = acc[...].astype(BF)
    lane = lax.broadcasted_iota(jnp.int32, (rows, stat_ref.shape[2]), 1)
    stat_ref[0] = jnp.where(lane == 0, top[:, :1], tot[:, :1])


def attend(flat_query, prompt_latent, own_rows, count, table, own, rank):
    samples, rows, latent = flat_query.shape
    prompt = prompt_latent.shape[0]
    return pl.pallas_call(
        attend_kernel,
        grid_spec=pltpu.PrefetchScalarGridSpec(
            num_scalar_prefetch=3,
            grid=(samples,),
            in_specs=[
                pl.BlockSpec((1, rows, latent), lambda s, *_: (s, 0, 0)),
                pl.BlockSpec((prompt, latent), lambda s, *_: (0, 0)),
                pl.BlockSpec((1, OWN_ROWS, latent), lambda s, *_: (s, 0, 0)),
            ],
            out_specs=[
                pl.BlockSpec((1, rows, rank), lambda s, *_: (s, 0, 0)),
                pl.BlockSpec((1, rows, 2), lambda s, *_: (s, 0, 0)),
            ],
            scratch_shapes=[
                pltpu.VMEM((PAIR, latent), BF),
                pltpu.VMEM((rows, rank), F32),
                pltpu.VMEM((rows, 128), F32),
                pltpu.VMEM((rows, 128), F32),
            ],
        ),
        out_shape=[
            jax.ShapeDtypeStruct((samples, rows, rank), BF),
            jax.ShapeDtypeStruct((samples, rows, 2), F32),
        ],
        compiler_params=pltpu.CompilerParams(vmem_limit_bytes=40 * 1024 * 1024),
        cost_estimate=pl.CostEstimate(
            flops=2 * samples * rows * PAIR * (latent + rank),
            bytes_accessed=2 * samples * rows * (latent + rank),
            transcendentals=samples * rows * PAIR,
        ),
    )(count, table, own, flat_query, prompt_latent, own_rows)


def per_device(
    queries,
    prompt_latent,
    new_latent,
    blocks,
    value_up,
    w_out,
    residual,
    norm_gain,
    router,
    routes,
    bucket_slots,
    w_gate,
    w_up,
    w_down,
):
    n_ctx = lax.axis_size("ctx")
    n_ep = lax.axis_size("ep")
    devices = n_ctx * n_ep
    ctx_place = lax.axis_index("ctx")
    ep_place = lax.axis_index("ep")
    core = ep_place % 2
    swap = [(i, i ^ 1) for i in range(n_ep)]
    samples, step_count, head_count, latent = queries.shape
    rank = value_up.shape[1]
    value_width = value_up.shape[2]
    own_heads = head_count // n_ctx
    tokens_here = samples * step_count
    model_width = w_out.shape[1]
    part = model_width // n_ep

    all_up = lax.all_gather(value_up, ("ctx", "ep"), axis=0, tiled=True)

    blk_local = prompt_latent.shape[0] // BLOCK
    shard_of = blocks // blk_local
    offset = blocks % blk_local
    is_local = (shard_of == ctx_place).astype(jnp.int32)
    position = jnp.cumsum(is_local, axis=1) - 1
    chosen = (is_local[:, :, None] == 1) & (
        position[:, :, None] == jnp.arange(CAPB)[None, None, :]
    )
    table = jnp.sum(jnp.where(chosen, offset[:, :, None], 0), axis=1)
    count = jnp.minimum(jnp.sum(is_local, axis=1), CAPB)
    own = (ctx_place == n_ctx - 1).astype(jnp.int32).reshape(1)
    own_rows = jnp.pad(new_latent, ((0, 0), (0, OWN_ROWS - step_count), (0, 0)))

    flat_query = queries.reshape(samples, step_count * head_count, latent)
    acc, stat = attend(flat_query, prompt_latent, own_rows, count, table, own, rank)

    stat = stat.reshape(samples, step_count, n_ctx, own_heads, 2).transpose(2, 4, 3, 0, 1)
    stat = stat.reshape(n_ctx, 2 * own_heads, tokens_here)
    stat = lax.all_to_all(stat, "ctx", split_axis=0, concat_axis=0, tiled=True)
    row_max, row_total = stat[:, :own_heads], stat[:, own_heads:]
    factor = jnp.exp(row_max - jnp.max(row_max, axis=0, keepdims=True))
    factor = factor / jnp.sum(factor * row_total, axis=0, keepdims=True)

    w_cols = w_out.reshape(w_out.shape[0], n_ep, part).transpose(1, 0, 2)
    w_cols = lax.all_to_all(w_cols, "ep", split_axis=0, concat_axis=0, tiled=True)
    w_cols = w_cols.reshape(own_heads * value_width, part)

    acc = acc.reshape(samples, step_count, head_count, rank)
    part_values = jnp.einsum("sthr,hrv->hstv", acc, all_up, preferred_element_type=F32).astype(BF)
    part_values = part_values.reshape(n_ctx, own_heads * tokens_here, value_width)
    part_values = lax.all_to_all(part_values, "ctx", split_axis=0, concat_axis=0, tiled=True)
    part_values = part_values.reshape(n_ctx, own_heads, tokens_here, value_width)
    head_values = jnp.sum(part_values.astype(F32) * factor[..., None], axis=0).astype(BF)
    head_values = head_values.transpose(1, 0, 2).reshape(tokens_here, own_heads * value_width)

    head_flat = lax.all_gather(head_values, "ep", axis=0, tiled=True)
    projected = jnp.dot(head_flat, w_cols, preferred_element_type=F32).astype(BF)
    tok_dev = residual.shape[0]
    projected = lax.all_to_all(
        projected.reshape(devices, tok_dev, part),
        ("ctx", "ep"),
        split_axis=0,
        concat_axis=0,
        tiled=True,
    )
    attention = jnp.sum(projected.reshape(n_ctx, n_ep, tok_dev, part).astype(F32), axis=0)
    attention = attention.transpose(1, 0, 2).reshape(tok_dev, model_width)

    hidden_state = (residual.astype(F32) + attention).astype(BF)
    hidden_wide = hidden_state.astype(F32)
    mean_square = jnp.mean(hidden_wide * hidden_wide, axis=1, keepdims=True)
    normed = (hidden_wide * lax.rsqrt(mean_square + 1e-06) * norm_gain).astype(BF)
    affinity = jax.nn.sigmoid(jnp.dot(normed, router, preferred_element_type=F32))
    experts_all = router.shape[1]
    experts = jnp.arange(experts_all)
    picked = (routes[:, :, None] == experts[None, None, :]).astype(F32)
    picked_aff = jnp.sum(picked * affinity[:, None, :], axis=2)
    combine_w = 2.5 * picked_aff / jnp.sum(picked_aff, axis=1, keepdims=True)
    kept_route = bucket_slots < CAP
    hits = picked[:, :, :, None] * (
        (bucket_slots[:, :, None] == jnp.arange(CAP)[None, None, :]) & kept_route[:, :, None]
    ).astype(F32)[:, :, None, :]
    slot_hit = jnp.sum(hits, axis=1).reshape(tok_dev, experts_all * CAP)
    slot_weight = jnp.sum(hits * combine_w[:, :, None, None], axis=1)

    outgoing = jnp.einsum(
        "te,td->ed", slot_hit.astype(BF), normed, preferred_element_type=F32
    ).astype(BF)
    chips = n_ep // CAP
    copies = jnp.broadcast_to(
        outgoing.reshape(n_ctx, 1, CAP, n_ep, part), (n_ctx, chips, CAP, n_ep, part)
    ).reshape(devices, n_ep, part)
    arrived = lax.all_to_all(copies, ("ctx", "ep"), split_axis=0, concat_axis=0, tiled=True)
    arrived = arrived.reshape(devices, model_width)
    sibling = lax.ppermute(arrived, "ep", swap)
    rows = jnp.concatenate([arrived, sibling], axis=0)
    gate_act = jnp.dot(rows, w_gate[0], preferred_element_type=F32)
    up_act = jnp.dot(rows, w_up[0], preferred_element_type=F32)
    inner_act = (jax.nn.silu(gate_act) * up_act).astype(BF)
    theirs = jnp.dot(inner_act[devices:], w_down[0], preferred_element_type=F32).astype(BF)
    theirs = lax.ppermute(theirs, "ep", swap)
    ours = jnp.dot(inner_act[:devices], w_down[0], preferred_element_type=F32)
    pair_out = (ours + theirs.astype(F32)).astype(BF).reshape(devices, n_ep, part)
    returned = lax.all_to_all(pair_out, ("ctx", "ep"), split_axis=0, concat_axis=0, tiled=True)
    expert_rows = jnp.sum(
        returned.reshape(n_ctx, chips, CAP, n_ep, part).astype(F32), axis=1
    ).reshape(1, experts_all, CAP, n_ep, part)
    moe_sum = jnp.sum(slot_weight[:, :, :, None, None] * expert_rows, axis=(1, 2))
    return (hidden_wide + moe_sum.reshape(tok_dev, model_width)).astype(BF)


def solution(mesh):
    placed = (
        P("ep", None, None, None),
        P("ctx", None),
        P("ep", None, None),
        P("ep", None),
        P(("ctx", "ep"), None, None),
        P(("ctx", "ep"), None),
        P(("ctx", "ep"), None),
        P(),
        P(),
        P(("ctx", "ep"), None),
        P(("ctx", "ep"), None),
        P("ctx", None, "ep"),
        P("ctx", None, "ep"),
        P("ctx", "ep", None),
    )
    return jax.shard_map(
        per_device, mesh=mesh, in_specs=placed, out_specs=P(("ctx", "ep"), None), check_vma=False
    )
```

```python
import functools

import jax
import jax.numpy as jnp
from jax import lax
from jax.experimental import pallas as pl
from jax.experimental.pallas import tpu as pltpu
from jax.sharding import PartitionSpec as P

BLOCK = 64
CAPB = 8
CAP = 2
FEW = 2
GROUP = 4
RING = 4
STAT_ROWS = 16
VMEM_LIMIT = 40 * 1024 * 1024
OWN_ROWS = 16

score_scale = 192.0 ** (-0.5)
masked_score = -1e30
BF = jnp.bfloat16
F32 = jnp.float32


def cut(ref, place, spans, lead=()):
    pieces = [
        ref[(*lead, pl.ds(pl.multiple_of(base + place * width, 8), width), slice(None))]
        for base, width in spans
    ]
    return jnp.concatenate(pieces, axis=0)


def split(value):
    high = value.astype(BF)
    rest = value - high.astype(F32)
    middle = rest.astype(BF)
    return high, middle, (rest - middle.astype(F32)).astype(BF)


def attend_kernel(
    count_ref, table_ref, info_ref, q_ref, prompt_ref, new_ref, *refs, spans, offset
):
    *out_refs, few, many, acc, stat = refs
    group, steps, latent, heads = q_ref.shape
    rank = out_refs[0].shape[2]
    rows = steps * heads
    first = offset + pl.program_id(0) * group
    own = info_ref[0]
    place = info_ref[1]

    def one(g, keys, n_blocks):
        sample = first + g
        count = count_ref[sample]
        for j in range(n_blocks):
            start = pl.multiple_of(table_ref[sample, j] * BLOCK, BLOCK)
            keys[j * BLOCK : (j + 1) * BLOCK, :] = prompt_ref[pl.ds(start, BLOCK), :]
        n_prompt = n_blocks * BLOCK
        keys[n_prompt : n_prompt + OWN_ROWS, :] = new_ref[g]
        n_keys = n_prompt + OWN_ROWS
        query = jnp.concatenate([q_ref[g, t] for t in range(steps)], axis=1)
        scores = jnp.dot(keys[...], query, preferred_element_type=F32) * score_scale
        key = lax.broadcasted_iota(jnp.int32, (n_keys, rows), 0)
        step = (lax.broadcasted_iota(jnp.int32, (n_keys, rows), 1) >= heads).astype(jnp.int32)
        own_last = jnp.where(own == 1, n_prompt + step, -1)
        live = (key < count * BLOCK) | ((key >= n_prompt) & (key <= own_last))
        scores = jnp.where(live, scores, masked_score)
        top = jnp.max(scores, axis=0, keepdims=True)
        weight = jnp.exp(scores - top)
        stat[g : g + 1, :rows] = top
        stat[g : g + 1, rows:] = jnp.sum(weight, axis=0, keepdims=True)
        acc[g] = lax.dot_general(
            weight.astype(BF),
            keys[:, :rank],
            (((0,), (0,)), ((), ())),
            preferred_element_type=F32,
        )
        part_rows = rows // RING
        late = (pl.program_id(0) >= pl.num_programs(0) // 2).astype(jnp.int32)
        for k, out_ref in zip((0, 2 - late, 3 - late, 1 + 2 * late), out_refs):
            part = cut(acc, lax.rem(place + k, RING), spans, (g,))
            out_ref[0, g * part_rows : (g + 1) * part_rows, :] = part.astype(BF)

    for g in range(group):
        one(g, few.at[g], FEW)
    for g in range(group):

        @pl.when(count_ref[first + g] > FEW)
        def _():
            one(g, many, CAPB)

    for i, addend in enumerate(split(stat[0:group, :])):
        stat[(i + 1) * group : (i + 2) * group, :] = addend.astype(F32)
    stat[4 * group :, :] = jnp.zeros((STAT_ROWS - 3 * group, 2 * rows), F32)
    tail = stat[group : group + STAT_ROWS, :].astype(BF)
    for out_ref in out_refs:
        out_ref[0, group * rows // RING :, :] = tail


def attend(query_t, prompt_latent, own_rows, count, table, info, rank, half, spans):
    samples, steps, latent, heads = query_t.shape
    samples = samples // 2
    rows = steps * heads
    prompt = prompt_latent.shape[0]
    groups = samples // GROUP
    skip = half * groups
    part_rows = GROUP * rows // RING + STAT_ROWS
    return pl.pallas_call(
        functools.partial(attend_kernel, spans=spans, offset=half * samples),
        grid_spec=pltpu.PrefetchScalarGridSpec(
            num_scalar_prefetch=3,
            grid=(groups,),
            in_specs=[
                pl.BlockSpec((GROUP, steps, latent, heads), lambda s, *_: (s + skip, 0, 0, 0)),
                pl.BlockSpec((prompt, latent), lambda s, *_: (0, 0)),
                pl.BlockSpec((GROUP, OWN_ROWS, latent), lambda s, *_: (s + skip, 0, 0)),
            ],
            out_specs=[pl.BlockSpec((1, part_rows, rank), lambda s, *_: (s, 0, 0))] * RING,
            scratch_shapes=[
                pltpu.VMEM((GROUP, FEW * BLOCK + OWN_ROWS, latent), BF),
                pltpu.VMEM((CAPB * BLOCK + OWN_ROWS, latent), BF),
                pltpu.VMEM((GROUP, rows, rank), F32),
                pltpu.VMEM((GROUP + STAT_ROWS, 2 * rows), F32),
            ],
        ),
        out_shape=[jax.ShapeDtypeStruct((groups, part_rows, rank), BF)] * RING,
        compiler_params=pltpu.CompilerParams(vmem_limit_bytes=VMEM_LIMIT),
        cost_estimate=pl.CostEstimate(
            flops=4 * samples * rows * FEW * BLOCK * (latent + rank),
            bytes_accessed=4 * samples * rows * (latent + rank),
            transcendentals=samples * rows * FEW * BLOCK,
        ),
    )(count, table, info, query_t, prompt_latent, own_rows)


def columns_of(stats, scratch, place, spans, total_base):
    lanes = scratch.shape[1]
    row = lax.broadcasted_iota(jnp.int32, (STAT_ROWS, lanes), 0)
    lane = lax.broadcasted_iota(jnp.int32, (STAT_ROWS, lanes), 1)
    pick = ((row % GROUP == lane) & (row < 3 * GROUP)).astype(BF)
    scratch[...] = lax.dot_general(
        stats, pick, (((0,), (0,)), ((), ())), preferred_element_type=F32
    )
    totals = [(base + total_base, width) for base, width in spans]
    return cut(scratch, place, spans), cut(scratch, place, totals)


def combined(parts, scratch, place, spans, total_base):
    body = parts[0].shape[0] - STAT_ROWS
    stats = [
        columns_of(part[body:, :], scratch.at[k], place, spans, total_base)
        for k, part in enumerate(parts)
    ]
    top = functools.reduce(jnp.maximum, [one for one, _ in stats])
    factors = [jnp.exp(one - top) for one, _ in stats]
    return top, sum(f * one for f, (_, one) in zip(factors, stats)), factors


def weighted(parts, factors, j):
    rows = factors[0].shape[0]
    return sum(
        part[j * rows : (j + 1) * rows, :].astype(F32) * factor[:, j : j + 1]
        for part, factor in zip(parts, factors)
    )


def stat_tail(scratch, addends):
    for i, addend in enumerate(addends):
        scratch[i * GROUP : (i + 1) * GROUP, :] = addend.astype(F32)
    scratch[3 * GROUP :, :] = jnp.zeros((STAT_ROWS - 3 * GROUP, scratch.shape[1]), F32)
    return scratch[...].astype(BF)


def relay_kernel(place_ref, held, ahead, behind, forward, backward, columns, lines, *, spans):
    body = held.shape[2] - STAT_ROWS
    half_width = lines.shape[2] // 2
    for side, (passed, out, k) in enumerate(((ahead, forward, 1), (behind, backward, 3))):
        parts = [held.at[side, 0], passed.at[side, 0]]
        target = lax.rem(place_ref[0] + k, RING)
        _, _, factors = combined(parts, columns, target, spans, half_width)
        for j in range(GROUP):
            rows = body // GROUP
            out[0, j * rows : (j + 1) * rows, :] = weighted(parts, factors, j).astype(BF)
        both = []
        for k, part in enumerate(parts):
            lines[k] = part[body:, :].astype(F32)
            both.append(sum(lines[k, i * GROUP : (i + 1) * GROUP, :] for i in range(3)))
        tops = [one[:, :half_width] for one in both]
        top = jnp.maximum(*tops)
        total = sum(jnp.exp(t - top) * one[:, half_width:] for t, one in zip(tops, both))
        addends = split(jnp.concatenate([top, total], axis=1))
        out[0, body:, :] = stat_tail(lines.at[0], addends)


def relay(held, ahead, behind, place, spans):
    groups, part_rows, rank = held.shape
    paired = (2, groups // 2, part_rows, rank)
    both = pl.BlockSpec((2, 1, part_rows, rank), lambda s, *_: (0, s, 0, 0))
    return pl.pallas_call(
        functools.partial(relay_kernel, spans=spans),
        grid_spec=pltpu.PrefetchScalarGridSpec(
            num_scalar_prefetch=1,
            grid=(groups // 2,),
            in_specs=[both] * 3,
            out_specs=[pl.BlockSpec((1, part_rows, rank), lambda s, *_: (s, 0, 0))] * 2,
            scratch_shapes=[
                pltpu.VMEM((2, rank, 128), F32),
                pltpu.VMEM((2, STAT_ROWS, rank), F32),
            ],
        ),
        out_shape=[jax.ShapeDtypeStruct((groups // 2, part_rows, rank), BF)] * 2,
        compiler_params=pltpu.CompilerParams(vmem_limit_bytes=VMEM_LIMIT),
        cost_estimate=pl.CostEstimate(
            flops=4 * groups * part_rows * rank,
            bytes_accessed=6 * groups * part_rows * rank,
            transcendentals=0,
        ),
    )(place, held.reshape(paired), ahead.reshape(paired), behind.reshape(paired))


def first_kernel(
    place_ref, own, ahead, behind, passed_f, passed_b, *refs, spans, next_spans
):
    *outs, columns, total, stat = refs
    rows = sum(width for _, width in spans)
    width = stat.shape[1]
    for side, parts in enumerate(
        (
            [own.at[0, 0], passed_f.at[0], behind.at[0, 0]],
            [own.at[1, 0], passed_b.at[0], ahead.at[1, 0]],
        )
    ):
        top, tot, factors = combined(parts, columns, place_ref[0], spans, width // 2)
        for j in range(GROUP):
            total[j * rows : (j + 1) * rows, :] = weighted(parts, factors, j)
        row = lax.broadcasted_iota(jnp.int32, (rows, width), 0)
        lane = lax.broadcasted_iota(jnp.int32, (rows, width), 1)
        addends = [
            sum(
                lax.dot_general(
                    value,
                    (lane == row + base).astype(BF),
                    (((0,), (0,)), ((), ())),
                    preferred_element_type=F32,
                )
                for value, base in ((one, 0), (other, rows))
            )[:GROUP, :]
            for one, other in zip(split(top), split(tot))
        ]
        tail = stat_tail(stat, addends)
        small = GROUP * rows // RING
        for k, out in enumerate(outs):
            target = lax.rem(place_ref[1] + k, RING)
            every = [(j * rows + base, w) for j in range(GROUP) for base, w in next_spans]
            out[side, 0, :small, :] = cut(total, target, every).astype(BF)
            out[side, 0, small:, :] = tail


def first_merge(own, ahead, behind, passed_f, passed_b, places, spans, next_spans):
    groups, part_rows, rank = own.shape
    rows = sum(width for _, width in spans)
    paired = (2, groups // 2, part_rows, rank)
    out_rows = GROUP * rows // RING + STAT_ROWS
    both = pl.BlockSpec((2, 1, part_rows, rank), lambda s, *_: (0, s, 0, 0))
    single = pl.BlockSpec((1, part_rows, rank), lambda s, *_: (s, 0, 0))
    outs = pl.pallas_call(
        functools.partial(first_kernel, spans=spans, next_spans=next_spans),
        grid_spec=pltpu.PrefetchScalarGridSpec(
            num_scalar_prefetch=1,
            grid=(groups // 2,),
            in_specs=[both] * 3 + [single] * 2,
            out_specs=[pl.BlockSpec((2, 1, out_rows, rank), lambda s, *_: (0, s, 0, 0))] * RING,
            scratch_shapes=[
                pltpu.VMEM((3, rank, 128), F32),
                pltpu.VMEM((GROUP * rows, rank), F32),
                pltpu.VMEM((STAT_ROWS, rank), F32),
            ],
        ),
        out_shape=[jax.ShapeDtypeStruct((2, groups // 2, out_rows, rank), BF)] * RING,
        compiler_params=pltpu.CompilerParams(vmem_limit_bytes=VMEM_LIMIT),
        cost_estimate=pl.CostEstimate(
            flops=6 * groups * part_rows * rank,
            bytes_accessed=8 * groups * part_rows * rank,
            transcendentals=0,
        ),
    )(
        places,
        own.reshape(paired),
        ahead.reshape(paired),
        behind.reshape(paired),
        passed_f,
        passed_b,
    )
    return [out.reshape(groups, out_rows, rank) for out in outs]


def last_kernel(place_ref, *refs, spans, total_base):
    *parts, out, columns = refs
    parts = [part.at[0] for part in parts]
    _, total, factors = combined(parts, columns, place_ref[0], spans, total_base)
    factors = [factor / total for factor in factors]
    rows = factors[0].shape[0]
    for j in range(GROUP):
        out[0, j * rows : (j + 1) * rows, :] = weighted(parts, factors, j).astype(BF)


def last_merge(parts, place, spans, total_base):
    groups, part_rows, rank = parts[0].shape
    out_rows = part_rows - STAT_ROWS
    return pl.pallas_call(
        functools.partial(last_kernel, spans=spans, total_base=total_base),
        grid_spec=pltpu.PrefetchScalarGridSpec(
            num_scalar_prefetch=1,
            grid=(groups,),
            in_specs=[pl.BlockSpec((1, part_rows, rank), lambda s, *_: (s, 0, 0))] * RING,
            out_specs=pl.BlockSpec((1, out_rows, rank), lambda s, *_: (s, 0, 0)),
            scratch_shapes=[pltpu.VMEM((RING, rank, 128), F32)],
        ),
        out_shape=jax.ShapeDtypeStruct((groups, out_rows, rank), BF),
        compiler_params=pltpu.CompilerParams(vmem_limit_bytes=VMEM_LIMIT),
        cost_estimate=pl.CostEstimate(
            flops=8 * groups * part_rows * rank,
            bytes_accessed=10 * groups * part_rows * rank,
            transcendentals=0,
        ),
    )(place, *parts)


def per_device(
    queries,
    prompt_latent,
    new_latent,
    blocks,
    value_up,
    w_out,
    residual,
    norm_gain,
    router,
    routes,
    bucket_slots,
    w_gate,
    w_up,
    w_down,
):
    n_ctx = lax.axis_size("ctx")
    n_ep = lax.axis_size("ep")
    devices = n_ctx * n_ep
    ctx_place = lax.axis_index("ctx")
    ep_place = lax.axis_index("ep")
    core = ep_place % 2
    swap = [(i, i ^ 1) for i in range(n_ep)]
    samples, step_count, head_count, latent = queries.shape
    rank = value_up.shape[1]
    value_width = value_up.shape[2]
    own_heads = head_count // n_ctx
    tokens_here = samples * step_count
    model_width = w_out.shape[1]
    part = model_width // n_ep

    w_rows = lax.all_gather(
        w_out,
        "ep",
        axis=0,
        axis_index_groups=[list(range(k, n_ep, 2)) for k in range(2)],
        tiled=True,
    )
    z_place, y_place = ctx_place // RING, ctx_place % RING
    ctx_axes = jnp.stack([z_place, y_place])

    inward = [(e * n_ctx + c, c * n_ep + e) for e in range(n_ep) for c in range(n_ctx)]
    outward = [(there, here) for here, there in inward]
    everywhere = ("ctx", "ep")
    residual, routes, bucket_slots = (
        lax.ppermute(value, everywhere, inward) for value in (residual, routes, bucket_slots)
    )

    def along_z(k):
        return [(i, (i + k * RING) % n_ctx) for i in range(n_ctx)]

    def along_y(k):
        return [(i, i // RING * RING + (i + k) % RING) for i in range(n_ctx)]

    blk_local = prompt_latent.shape[0] // BLOCK
    shard_of = blocks // blk_local
    offset = blocks % blk_local
    is_local = (shard_of == ctx_place).astype(jnp.int32)
    position = jnp.cumsum(is_local, axis=1) - 1
    chosen = (is_local[:, :, None] == 1) & (
        position[:, :, None] == jnp.arange(CAPB)[None, None, :]
    )
    table = jnp.sum(jnp.where(chosen, offset[:, :, None], 0), axis=1)
    count = jnp.minimum(jnp.sum(is_local, axis=1), CAPB)
    own = (ctx_place == n_ctx - 1).astype(jnp.int32)
    own_rows = jnp.pad(new_latent, ((0, 0), (0, OWN_ROWS - step_count), (0, 0)))

    query_t = jnp.swapaxes(queries, 2, 3)
    per_step = head_count // RING
    by_z = [(t * head_count, per_step) for t in range(step_count)]
    by_y = [
        (t * head_count + z * per_step, own_heads) for t in range(step_count) for z in range(RING)
    ]
    second = [(t * per_step, own_heads) for t in range(step_count)]
    part_rows = step_count * per_step

    def send(forward, backward, along):
        return lax.ppermute(forward, "ctx", along(1)), lax.ppermute(backward, "ctx", along(3))

    z_first, y_first = ctx_axes, ctx_axes[::-1]
    own_a, forward_a, backward_a, held_a = attend(
        query_t, prompt_latent, own_rows, count, table, jnp.stack([own, z_place]), rank, 0, by_z
    )
    ahead_a, behind_a = send(forward_a, backward_a, along_z)
    own_b, forward_b, backward_b, held_b = attend(
        query_t, prompt_latent, own_rows, count, table, jnp.stack([own, y_place]), rank, 1, by_y
    )
    ahead_b, behind_b = send(forward_b, backward_b, along_y)
    passed_a = relay(held_a, ahead_a, behind_a, z_first, by_z)
    passed_fa, passed_ba = send(*passed_a, along_z)
    passed_b = relay(held_b, ahead_b, behind_b, y_first, by_y)
    passed_fb, passed_bb = send(*passed_b, along_y)

    value_up, _ = lax.optimization_barrier((value_up, passed_b[0]))
    own_up = lax.all_to_all(
        jnp.broadcast_to(value_up, (n_ep,) + value_up.shape[1:]),
        "ep",
        split_axis=0,
        concat_axis=0,
        tiled=True,
    )
    own_a, own_up = lax.optimization_barrier((own_a, own_up))

    next_a = first_merge(
        own_a, ahead_a, behind_a, passed_fa, passed_ba, z_first, by_z, second
    )
    next_b = first_merge(
        own_b, ahead_b, behind_b, passed_fb, passed_bb, y_first, by_y, second
    )
    got_a = [next_a[0]] + [lax.ppermute(next_a[k], "ctx", along_y(k)) for k in (1, 2, 3)]
    got_b = [next_b[0]] + [lax.ppermute(next_b[k], "ctx", along_z(k)) for k in (1, 2, 3)]
    latent_a = last_merge(got_a, y_first, second, part_rows)
    latent_b = last_merge(got_b, z_first, second, part_rows)
    latent_out = jnp.concatenate([latent_a, latent_b], axis=0)
    latent_out = latent_out.reshape(samples, step_count, own_heads, rank)
    head_values = jnp.einsum(
        "sthr,hrv->sthv", latent_out, own_up, preferred_element_type=F32
    ).astype(BF)
    head_values = head_values.reshape(tokens_here, own_heads // 2, 2, value_width)

    def pick(value, index, axis):
        return lax.dynamic_index_in_dim(value, index, axis, keepdims=False)

    kept = pick(head_values, core, 2)
    given = lax.ppermute(pick(head_values, 1 - core, 2), "ep", swap)
    head_flat = jnp.where(core == 0, jnp.stack([kept, given]), jnp.stack([given, kept]))
    theirs = jnp.dot(
        pick(head_flat, 1 - core, 0).reshape(tokens_here, -1), w_rows, preferred_element_type=F32
    ).astype(BF)
    theirs = lax.ppermute(theirs, "ep", swap)
    ours = jnp.dot(
        pick(head_flat, core, 0).reshape(tokens_here, -1), w_rows, preferred_element_type=F32
    )
    projected = (ours + theirs.astype(F32)).astype(BF)
    tok_dev = residual.shape[0]
    projected = lax.all_to_all(
        projected.reshape(n_ctx, tok_dev, model_width),
        "ctx",
        split_axis=0,
        concat_axis=0,
        tiled=True,
    )
    attention = jnp.sum(projected.astype(F32), axis=0)

    hidden_state = (residual.astype(F32) + attention).astype(BF)
    hidden_wide = hidden_state.astype(F32)
    mean_square = jnp.mean(hidden_wide * hidden_wide, axis=1, keepdims=True)
    normed = (hidden_wide * lax.rsqrt(mean_square + 1e-06) * norm_gain).astype(BF)
    affinity = jax.nn.sigmoid(jnp.dot(normed, router, preferred_element_type=F32))
    experts_all = router.shape[1]
    experts = jnp.arange(experts_all)
    picked = (routes[:, :, None] == experts[None, None, :]).astype(F32)
    picked_aff = jnp.sum(picked * affinity[:, None, :], axis=2)
    combine_w = 2.5 * picked_aff / jnp.sum(picked_aff, axis=1, keepdims=True)
    kept_route = bucket_slots < CAP
    hits = picked[:, :, :, None] * (
        (bucket_slots[:, :, None] == jnp.arange(CAP)[None, None, :]) & kept_route[:, :, None]
    ).astype(F32)[:, :, None, :]
    slot_hit = jnp.sum(hits, axis=1).reshape(tok_dev, experts_all * CAP)
    slot_weight = jnp.sum(hits * combine_w[:, :, None, None], axis=1)
    slot_weight = lax.ppermute(
        slot_weight.reshape(tok_dev, experts_all * CAP), everywhere, outward
    ).reshape(tok_dev, experts_all, CAP)
    hidden_wide = lax.ppermute(hidden_state, everywhere, outward).astype(F32)

    outgoing = jnp.einsum(
        "te,td->ed", slot_hit.astype(BF), normed, preferred_element_type=F32
    ).astype(BF)
    chips = n_ep // CAP
    copies = jnp.broadcast_to(
        outgoing.reshape(n_ctx, 1, CAP, n_ep, part), (n_ctx, chips, CAP, n_ep, part)
    ).reshape(devices, n_ep, part)
    arrived = lax.all_to_all(copies, ("ctx", "ep"), split_axis=0, concat_axis=0, tiled=True)
    arrived = arrived.reshape(devices, model_width)
    sibling = lax.ppermute(arrived, "ep", swap)
    rows = jnp.concatenate([arrived, sibling], axis=0)
    gate_act = jnp.dot(rows, w_gate[0], preferred_element_type=F32)
    up_act = jnp.dot(rows, w_up[0], preferred_element_type=F32)
    inner_act = (jax.nn.silu(gate_act) * up_act).astype(BF)
    theirs = jnp.dot(inner_act[devices:], w_down[0], preferred_element_type=F32).astype(BF)
    theirs = lax.ppermute(theirs, "ep", swap)
    ours = jnp.dot(inner_act[:devices], w_down[0], preferred_element_type=F32)
    pair_out = (ours + theirs.astype(F32)).astype(BF).reshape(n_ctx, n_ep, n_ep, part)
    pair_out = pair_out.swapaxes(0, 1).reshape(devices, n_ep, part)
    returned = lax.all_to_all(pair_out, ("ctx", "ep"), split_axis=0, concat_axis=0, tiled=True)
    expert_rows = jnp.sum(
        returned.reshape(n_ctx, chips, CAP, n_ep, part).astype(F32), axis=1
    ).reshape(1, experts_all, CAP, n_ep, part)
    moe_sum = jnp.sum(slot_weight[:, :, :, None, None] * expert_rows, axis=(1, 2))
    return (hidden_wide + moe_sum.reshape(tok_dev, model_width)).astype(BF)


def solution(mesh):
    placed = (
        P("ep", None, None, None),
        P("ctx", None),
        P("ep", None, None),
        P("ep", None),
        P(("ctx", "ep"), None, None),
        P(("ctx", "ep"), None),
        P(("ctx", "ep"), None),
        P(),
        P(),
        P(("ctx", "ep"), None),
        P(("ctx", "ep"), None),
        P("ctx", None, "ep"),
        P("ctx", None, "ep"),
        P("ctx", "ep", None),
    )
    return jax.shard_map(
        per_device, mesh=mesh, in_specs=placed, out_specs=P(("ctx", "ep"), None), check_vma=False
    )
```

```python
import functools

import jax
import jax.numpy as jnp
from jax import lax
from jax.experimental import pallas as pl
from jax.experimental.pallas import tpu as pltpu
from jax.sharding import PartitionSpec as P

BLOCK = 64
CAPB = 8
CAP = 2
FEW = 2
GROUP = 4
RING = 4
STAT_ROWS = 16
ATTEND_VMEM = 44 * 1024 * 1024
MERGE_VMEM = 12 * 1024 * 1024
OWN_ROWS = 16

score_scale = 192.0 ** (-0.5)
masked_score = -1e30
BF = jnp.bfloat16
F32 = jnp.float32


def cut(ref, place, spans, lead=()):
    pieces = [
        ref[(*lead, pl.ds(pl.multiple_of(base + place * width, 8), width), slice(None))]
        for base, width in spans
    ]
    return jnp.concatenate(pieces, axis=0)


def split(value):
    high = value.astype(BF)
    rest = value - high.astype(F32)
    middle = rest.astype(BF)
    return high, middle, (rest - middle.astype(F32)).astype(BF)


def attend_kernel(
    count_ref, table_ref, info_ref, q_ref, prompt_ref, new_ref, *refs, spans, offset
):
    *out_refs, few, many, acc, stat = refs
    group, steps, latent, heads = q_ref.shape
    rank = out_refs[0].shape[2]
    rows = steps * heads
    first = offset + pl.program_id(0) * group
    own = info_ref[0]
    place = info_ref[1]

    def one(g, keys, n_blocks):
        sample = first + g
        count = count_ref[sample]
        for j in range(n_blocks):
            start = pl.multiple_of(table_ref[sample, j] * BLOCK, BLOCK)
            keys[j * BLOCK : (j + 1) * BLOCK, :] = prompt_ref[pl.ds(start, BLOCK), :]
        n_prompt = n_blocks * BLOCK
        keys[n_prompt : n_prompt + OWN_ROWS, :] = new_ref[g]
        n_keys = n_prompt + OWN_ROWS
        query = jnp.concatenate([q_ref[g, t] for t in range(steps)], axis=1)
        scores = jnp.dot(keys[...], query, preferred_element_type=F32) * score_scale
        key = lax.broadcasted_iota(jnp.int32, (n_keys, rows), 0)
        step = (lax.broadcasted_iota(jnp.int32, (n_keys, rows), 1) >= heads).astype(jnp.int32)
        own_last = jnp.where(own == 1, n_prompt + step, -1)
        live = (key < count * BLOCK) | ((key >= n_prompt) & (key <= own_last))
        scores = jnp.where(live, scores, masked_score)
        top = jnp.max(scores, axis=0, keepdims=True)
        weight = jnp.exp(scores - top)
        stat[g : g + 1, :rows] = top
        stat[g : g + 1, rows:] = jnp.sum(weight, axis=0, keepdims=True)
        acc[g] = lax.dot_general(
            weight.astype(BF),
            keys[:, :rank],
            (((0,), (0,)), ((), ())),
            preferred_element_type=F32,
        )
        part_rows = rows // RING
        late = (pl.program_id(0) >= pl.num_programs(0) // 2).astype(jnp.int32)
        for k, out_ref in zip((0, 2 - late, 3 - late, 1 + 2 * late), out_refs):
            part = cut(acc, lax.rem(place + k, RING), spans, (g,))
            out_ref[0, g * part_rows : (g + 1) * part_rows, :] = part.astype(BF)

    for g in range(group):
        one(g, few.at[g], FEW)
    for g in range(group):

        @pl.when(count_ref[first + g] > FEW)
        def _():
            one(g, many, CAPB)

    for i, addend in enumerate(split(stat[0:group, :])):
        stat[(i + 1) * group : (i + 2) * group, :] = addend.astype(F32)
    stat[4 * group :, :] = jnp.zeros((STAT_ROWS - 3 * group, 2 * rows), F32)
    tail = stat[group : group + STAT_ROWS, :].astype(BF)
    for out_ref in out_refs:
        out_ref[0, group * rows // RING :, :] = tail


def attend(query_t, prompt_latent, own_rows, count, table, info, rank, half, spans):
    samples, steps, latent, heads = query_t.shape
    samples = samples // 2
    rows = steps * heads
    prompt = prompt_latent.shape[0]
    groups = samples // GROUP
    skip = half * groups
    part_rows = GROUP * rows // RING + STAT_ROWS
    return pl.pallas_call(
        functools.partial(attend_kernel, spans=spans, offset=half * samples),
        grid_spec=pltpu.PrefetchScalarGridSpec(
            num_scalar_prefetch=3,
            grid=(groups,),
            in_specs=[
                pl.BlockSpec((GROUP, steps, latent, heads), lambda s, *_: (s + skip, 0, 0, 0)),
                pl.BlockSpec((prompt, latent), lambda s, *_: (0, 0)),
                pl.BlockSpec((GROUP, OWN_ROWS, latent), lambda s, *_: (s + skip, 0, 0)),
            ],
            out_specs=[pl.BlockSpec((1, part_rows, rank), lambda s, *_: (s, 0, 0))] * RING,
            scratch_shapes=[
                pltpu.VMEM((GROUP, FEW * BLOCK + OWN_ROWS, latent), BF),
                pltpu.VMEM((CAPB * BLOCK + OWN_ROWS, latent), BF),
                pltpu.VMEM((GROUP, rows, rank), F32),
                pltpu.VMEM((GROUP + STAT_ROWS, 2 * rows), F32),
            ],
        ),
        out_shape=[pltpu.HBM((groups, part_rows, rank), BF)] * RING,
        compiler_params=pltpu.CompilerParams(vmem_limit_bytes=ATTEND_VMEM),
        cost_estimate=pl.CostEstimate(
            flops=4 * samples * rows * FEW * BLOCK * (latent + rank),
            bytes_accessed=4 * samples * rows * (latent + rank),
            transcendentals=samples * rows * FEW * BLOCK,
        ),
    )(count, table, info, query_t, prompt_latent, own_rows)


def columns_of(stats, scratch, place, spans, total_base):
    lanes = scratch.shape[1]
    row = lax.broadcasted_iota(jnp.int32, (STAT_ROWS, lanes), 0)
    lane = lax.broadcasted_iota(jnp.int32, (STAT_ROWS, lanes), 1)
    pick = ((row % GROUP == lane) & (row < 3 * GROUP)).astype(BF)
    scratch[...] = lax.dot_general(
        stats, pick, (((0,), (0,)), ((), ())), preferred_element_type=F32
    )
    totals = [(base + total_base, width) for base, width in spans]
    return cut(scratch, place, spans), cut(scratch, place, totals)


def combined(parts, scratch, place, spans, total_base):
    body = parts[0].shape[0] - STAT_ROWS
    stats = [
        columns_of(part[body:, :], scratch.at[k], place, spans, total_base)
        for k, part in enumerate(parts)
    ]
    top = functools.reduce(jnp.maximum, [one for one, _ in stats])
    factors = [jnp.exp(one - top) for one, _ in stats]
    return top, sum(f * one for f, (_, one) in zip(factors, stats)), factors


def weighted(parts, factors, j):
    rows = factors[0].shape[0]
    return sum(
        part[j * rows : (j + 1) * rows, :].astype(F32) * factor[:, j : j + 1]
        for part, factor in zip(parts, factors)
    )


def stat_tail(scratch, addends):
    for i, addend in enumerate(addends):
        scratch[i * GROUP : (i + 1) * GROUP, :] = addend.astype(F32)
    scratch[3 * GROUP :, :] = jnp.zeros((STAT_ROWS - 3 * GROUP, scratch.shape[1]), F32)
    return scratch[...].astype(BF)


def relay_kernel(place_ref, held, ahead, behind, forward, backward, columns, lines, *, spans):
    body = held.shape[2] - STAT_ROWS
    half_width = lines.shape[2] // 2
    for side, (passed, out, k) in enumerate(((ahead, forward, 1), (behind, backward, 3))):
        parts = [held.at[side, 0], passed.at[side, 0]]
        target = lax.rem(place_ref[0] + k, RING)
        _, _, factors = combined(parts, columns, target, spans, half_width)
        for j in range(GROUP):
            rows = body // GROUP
            out[0, j * rows : (j + 1) * rows, :] = weighted(parts, factors, j).astype(BF)
        both = []
        for k, part in enumerate(parts):
            lines[k] = part[body:, :].astype(F32)
            both.append(sum(lines[k, i * GROUP : (i + 1) * GROUP, :] for i in range(3)))
        tops = [one[:, :half_width] for one in both]
        top = jnp.maximum(*tops)
        total = sum(jnp.exp(t - top) * one[:, half_width:] for t, one in zip(tops, both))
        addends = split(jnp.concatenate([top, total], axis=1))
        out[0, body:, :] = stat_tail(lines.at[0], addends)


def relay(held, ahead, behind, place, spans):
    groups, part_rows, rank = held.shape
    paired = (2, groups // 2, part_rows, rank)
    both = pl.BlockSpec((2, 1, part_rows, rank), lambda s, *_: (0, s, 0, 0))
    return pl.pallas_call(
        functools.partial(relay_kernel, spans=spans),
        grid_spec=pltpu.PrefetchScalarGridSpec(
            num_scalar_prefetch=1,
            grid=(groups // 2,),
            in_specs=[both] * 3,
            out_specs=[pl.BlockSpec((1, part_rows, rank), lambda s, *_: (s, 0, 0))] * 2,
            scratch_shapes=[
                pltpu.VMEM((2, rank, 128), F32),
                pltpu.VMEM((2, STAT_ROWS, rank), F32),
            ],
        ),
        out_shape=[jax.ShapeDtypeStruct((groups // 2, part_rows, rank), BF)] * 2,
        compiler_params=pltpu.CompilerParams(vmem_limit_bytes=MERGE_VMEM),
        cost_estimate=pl.CostEstimate(
            flops=4 * groups * part_rows * rank,
            bytes_accessed=6 * groups * part_rows * rank,
            transcendentals=0,
        ),
    )(place, held.reshape(paired), ahead.reshape(paired), behind.reshape(paired))


def first_kernel(
    place_ref, own, ahead, behind, passed_f, passed_b, *refs, spans, next_spans
):
    *outs, columns, total, stat = refs
    rows = sum(width for _, width in spans)
    width = stat.shape[1]
    for side, parts in enumerate(
        (
            [own.at[0, 0], passed_f.at[0], behind.at[0, 0]],
            [own.at[1, 0], passed_b.at[0], ahead.at[1, 0]],
        )
    ):
        top, tot, factors = combined(parts, columns, place_ref[0], spans, width // 2)
        for j in range(GROUP):
            total[j * rows : (j + 1) * rows, :] = weighted(parts, factors, j)
        row = lax.broadcasted_iota(jnp.int32, (rows, width), 0)
        lane = lax.broadcasted_iota(jnp.int32, (rows, width), 1)
        addends = [
            sum(
                lax.dot_general(
                    value,
                    (lane == row + base).astype(BF),
                    (((0,), (0,)), ((), ())),
                    preferred_element_type=F32,
                )
                for value, base in ((one, 0), (other, rows))
            )[:GROUP, :]
            for one, other in zip(split(top), split(tot))
        ]
        tail = stat_tail(stat, addends)
        small = GROUP * rows // RING
        for k, out in enumerate(outs):
            target = lax.rem(place_ref[1] + k, RING)
            every = [(j * rows + base, w) for j in range(GROUP) for base, w in next_spans]
            out[side, 0, :small, :] = cut(total, target, every).astype(BF)
            out[side, 0, small:, :] = tail


def first_merge(own, ahead, behind, passed_f, passed_b, places, spans, next_spans):
    groups, part_rows, rank = own.shape
    rows = sum(width for _, width in spans)
    paired = (2, groups // 2, part_rows, rank)
    out_rows = GROUP * rows // RING + STAT_ROWS
    both = pl.BlockSpec((2, 1, part_rows, rank), lambda s, *_: (0, s, 0, 0))
    single = pl.BlockSpec((1, part_rows, rank), lambda s, *_: (s, 0, 0))
    outs = pl.pallas_call(
        functools.partial(first_kernel, spans=spans, next_spans=next_spans),
        grid_spec=pltpu.PrefetchScalarGridSpec(
            num_scalar_prefetch=1,
            grid=(groups // 2,),
            in_specs=[both] * 3 + [single] * 2,
            out_specs=[pl.BlockSpec((2, 1, out_rows, rank), lambda s, *_: (0, s, 0, 0))] * RING,
            scratch_shapes=[
                pltpu.VMEM((3, rank, 128), F32),
                pltpu.VMEM((GROUP * rows, rank), F32),
                pltpu.VMEM((STAT_ROWS, rank), F32),
            ],
        ),
        out_shape=[jax.ShapeDtypeStruct((2, groups // 2, out_rows, rank), BF)] * RING,
        compiler_params=pltpu.CompilerParams(vmem_limit_bytes=MERGE_VMEM),
        cost_estimate=pl.CostEstimate(
            flops=6 * groups * part_rows * rank,
            bytes_accessed=8 * groups * part_rows * rank,
            transcendentals=0,
        ),
    )(
        places,
        own.reshape(paired),
        ahead.reshape(paired),
        behind.reshape(paired),
        passed_f,
        passed_b,
    )
    return [out.reshape(groups, out_rows, rank) for out in outs]


def last_kernel(place_ref, *refs, spans, total_base):
    *parts, kept, given, columns = refs
    parts = [part.at[0] for part in parts]
    _, total, factors = combined(parts, columns, place_ref[0], spans, total_base)
    factors = [factor / total for factor in factors]
    value = jnp.concatenate([weighted(parts, factors, j) for j in range(GROUP)], axis=0)
    value = value.astype(BF)
    rows = value.shape[0]
    row = lax.broadcasted_iota(jnp.int32, (rows // 2, rows), 0)
    column = lax.broadcasted_iota(jnp.int32, (rows // 2, rows), 1)
    for out, core in ((kept, place_ref[1]), (given, 1 - place_ref[1])):
        every_second = (column == 2 * row + core).astype(BF)
        out[0] = jnp.dot(every_second, value, preferred_element_type=F32).astype(BF)


def last_merge(parts, place, core, spans, total_base):
    groups, part_rows, rank = parts[0].shape
    out_rows = (part_rows - STAT_ROWS) // 2
    return pl.pallas_call(
        functools.partial(last_kernel, spans=spans, total_base=total_base),
        grid_spec=pltpu.PrefetchScalarGridSpec(
            num_scalar_prefetch=1,
            grid=(groups,),
            in_specs=[pl.BlockSpec((1, part_rows, rank), lambda s, *_: (s, 0, 0))] * RING,
            out_specs=[pl.BlockSpec((1, out_rows, rank), lambda s, *_: (s, 0, 0))] * 2,
            scratch_shapes=[pltpu.VMEM((RING, rank, 128), F32)],
        ),
        out_shape=[jax.ShapeDtypeStruct((groups, out_rows, rank), BF)] * 2,
        compiler_params=pltpu.CompilerParams(vmem_limit_bytes=MERGE_VMEM),
        cost_estimate=pl.CostEstimate(
            flops=8 * groups * part_rows * rank,
            bytes_accessed=10 * groups * part_rows * rank,
            transcendentals=0,
        ),
    )(jnp.stack([place, core]), *parts)


def per_device(
    queries,
    prompt_latent,
    new_latent,
    blocks,
    value_up,
    w_out,
    residual,
    norm_gain,
    router,
    routes,
    bucket_slots,
    w_gate,
    w_up,
    w_down,
):
    n_ctx = lax.axis_size("ctx")
    n_ep = lax.axis_size("ep")
    devices = n_ctx * n_ep
    ctx_place = lax.axis_index("ctx")
    ep_place = lax.axis_index("ep")
    core = ep_place % 2
    swap = [(i, i ^ 1) for i in range(n_ep)]
    samples, step_count, head_count, latent = queries.shape
    rank = value_up.shape[1]
    value_width = value_up.shape[2]
    own_heads = head_count // n_ctx
    tokens_here = samples * step_count
    model_width = w_out.shape[1]
    part = model_width // n_ep

    same_core = [list(range(k, n_ep, 2)) for k in range(2)]
    w_rows = lax.all_gather(w_out, "ep", axis=0, axis_index_groups=same_core, tiled=True)
    z_place, y_place = ctx_place // RING, ctx_place % RING
    ctx_axes = jnp.stack([z_place, y_place])

    inward = [(e * n_ctx + c, c * n_ep + e) for e in range(n_ep) for c in range(n_ctx)]
    outward = [(there, here) for here, there in inward]
    everywhere = ("ctx", "ep")
    tok_dev, model_width = residual.shape

    chips = n_ep // 2
    up_rows = [value_up] + [
        lax.ppermute(value_up, "ep", [(i, (i + 2 * k) % n_ep) for i in range(n_ep)])
        for k in range(1, chips)
    ]
    ctx_axes, *up_rows = lax.optimization_barrier((ctx_axes, *up_rows))
    z_place, y_place = ctx_axes[0], ctx_axes[1]
    order = jnp.mod(ep_place // 2 - jnp.arange(chips), chips)
    up_rows = jnp.take(jnp.concatenate(up_rows, axis=0), order, axis=0)

    def along_z(k):
        return [(i, (i + k * RING) % n_ctx) for i in range(n_ctx)]

    def along_y(k):
        return [(i, i // RING * RING + (i + k) % RING) for i in range(n_ctx)]

    blk_local = prompt_latent.shape[0] // BLOCK
    shard_of = blocks // blk_local
    offset = blocks % blk_local
    is_local = (shard_of == ctx_place).astype(jnp.int32)
    position = jnp.cumsum(is_local, axis=1) - 1
    chosen = (is_local[:, :, None] == 1) & (
        position[:, :, None] == jnp.arange(CAPB)[None, None, :]
    )
    table = jnp.sum(jnp.where(chosen, offset[:, :, None], 0), axis=1)
    count = jnp.minimum(jnp.sum(is_local, axis=1), CAPB)
    own = (ctx_place == n_ctx - 1).astype(jnp.int32)
    own_rows = jnp.pad(new_latent, ((0, 0), (0, OWN_ROWS - step_count), (0, 0)))

    query_t = jnp.swapaxes(queries, 2, 3)
    per_step = head_count // RING
    by_z = [(t * head_count, per_step) for t in range(step_count)]
    by_y = [
        (t * head_count + z * per_step, own_heads) for t in range(step_count) for z in range(RING)
    ]
    second = [(t * per_step, own_heads) for t in range(step_count)]
    part_rows = step_count * per_step

    def send(forward, backward, along):
        return lax.ppermute(forward, "ctx", along(1)), lax.ppermute(backward, "ctx", along(3))

    z_first, y_first = ctx_axes, ctx_axes[::-1]
    own_a, forward_a, backward_a, held_a = attend(
        query_t, prompt_latent, own_rows, count, table, jnp.stack([own, z_place]), rank, 0, by_z
    )
    ahead_a, behind_a = send(forward_a, backward_a, along_z)
    own_b, forward_b, backward_b, held_b = attend(
        query_t, prompt_latent, own_rows, count, table, jnp.stack([own, y_place]), rank, 1, by_y
    )
    ahead_b, behind_b = send(forward_b, backward_b, along_y)
    passed_a = relay(held_a, ahead_a, behind_a, z_first, by_z)
    passed_fa, passed_ba = send(*passed_a, along_z)
    residual, _ = lax.optimization_barrier((residual, passed_a[0]))
    chosen_in = jnp.concatenate([residual, routes.astype(BF), bucket_slots.astype(BF)], axis=1)
    chosen_in = lax.ppermute(chosen_in, everywhere, inward)
    held_b, chosen_in = lax.optimization_barrier((held_b, chosen_in))
    residual = chosen_in[:, :model_width]
    routes, bucket_slots = jnp.split(chosen_in[:, model_width:].astype(jnp.int32), 2, axis=1)

    passed_b = relay(held_b, ahead_b, behind_b, y_first, by_y)
    passed_fb, passed_bb = send(*passed_b, along_y)

    next_a = first_merge(
        own_a, ahead_a, behind_a, passed_fa, passed_ba, z_first, by_z, second
    )
    next_b = first_merge(
        own_b, ahead_b, behind_b, passed_fb, passed_bb, y_first, by_y, second
    )
    got_a = [next_a[0]] + [lax.ppermute(next_a[k], "ctx", along_y(k)) for k in (1, 2, 3)]
    got_b = [next_b[0]] + [lax.ppermute(next_b[k], "ctx", along_z(k)) for k in (1, 2, 3)]
    latent_out = []
    for got, place in ((got_a, y_place), (got_b, z_place)):
        kept, given = last_merge(got, place, core, second, part_rows)
        latent_out.append(jnp.stack([kept, lax.ppermute(given, "ep", swap)]))
    latent_out = jnp.stack(latent_out, axis=1)
    latent_out = latent_out.reshape(2 * tokens_here, own_heads // 2, rank)
    head_values = jnp.einsum(
        "nhr,hrv->nhv", latent_out, up_rows, preferred_element_type=F32
    ).astype(BF)
    head_flat = head_values.reshape(2 * tokens_here, own_heads // 2 * value_width)
    projected = jnp.dot(head_flat, w_rows, preferred_element_type=F32).astype(BF)
    projected = lax.optimization_barrier(projected)
    ours = projected[:tokens_here].astype(F32)
    theirs = lax.ppermute(projected[tokens_here:], "ep", swap)
    projected = (ours + theirs.astype(F32)).astype(BF)
    projected = lax.all_to_all(
        projected.reshape(n_ctx, tok_dev, model_width),
        "ctx",
        split_axis=0,
        concat_axis=0,
        tiled=True,
    )
    attention = jnp.sum(projected.astype(F32), axis=0)

    hidden_state = (residual.astype(F32) + attention).astype(BF)
    hidden_wide = hidden_state.astype(F32)
    mean_square = jnp.mean(hidden_wide * hidden_wide, axis=1, keepdims=True)
    normed = (hidden_wide * lax.rsqrt(mean_square + 1e-06) * norm_gain).astype(BF)
    affinity = jax.nn.sigmoid(jnp.dot(normed, router, preferred_element_type=F32))
    experts_all = router.shape[1]
    experts = jnp.arange(experts_all)
    picked = (routes[:, :, None] == experts[None, None, :]).astype(F32)
    picked_aff = jnp.sum(picked * affinity[:, None, :], axis=2)
    combine_w = 2.5 * picked_aff / jnp.sum(picked_aff, axis=1, keepdims=True)
    kept_route = bucket_slots < CAP
    hits = picked[:, :, :, None] * (
        (bucket_slots[:, :, None] == jnp.arange(CAP)[None, None, :]) & kept_route[:, :, None]
    ).astype(F32)[:, :, None, :]
    slot_hit = jnp.sum(hits, axis=1).reshape(tok_dev, experts_all * CAP)
    slot_weight = jnp.sum(hits * combine_w[:, :, None, None], axis=1)
    slot_weight = lax.ppermute(
        slot_weight.reshape(tok_dev, experts_all * CAP), everywhere, outward
    ).reshape(tok_dev, experts_all, CAP)
    hidden_wide = lax.ppermute(hidden_state, everywhere, outward).astype(F32)

    outgoing = jnp.einsum(
        "te,td->ed", slot_hit.astype(BF), normed, preferred_element_type=F32
    ).astype(BF)
    copies = jnp.broadcast_to(
        outgoing.reshape(n_ctx, 1, CAP, n_ep, part), (n_ctx, chips, CAP, n_ep, part)
    ).reshape(devices, n_ep, part)
    arrived = lax.all_to_all(copies, ("ctx", "ep"), split_axis=0, concat_axis=0, tiled=True)
    arrived = arrived.reshape(devices, model_width)
    sibling = lax.ppermute(arrived, "ep", swap)
    rows = jnp.concatenate([arrived, sibling], axis=0)
    gate_act = jnp.dot(rows, w_gate[0], preferred_element_type=F32)
    up_act = jnp.dot(rows, w_up[0], preferred_element_type=F32)
    inner_act = (jax.nn.silu(gate_act) * up_act).astype(BF)
    theirs = jnp.dot(inner_act[devices:], w_down[0], preferred_element_type=F32).astype(BF)
    theirs = lax.ppermute(theirs, "ep", swap)
    ours = jnp.dot(inner_act[:devices], w_down[0], preferred_element_type=F32)
    pair_out = (ours + theirs.astype(F32)).astype(BF).reshape(n_ctx, n_ep, n_ep, part)
    pair_out = pair_out.swapaxes(0, 1).reshape(devices, n_ep, part)
    returned = lax.all_to_all(pair_out, ("ctx", "ep"), split_axis=0, concat_axis=0, tiled=True)
    expert_rows = jnp.sum(
        returned.reshape(n_ctx, chips, CAP, n_ep, part).astype(F32), axis=1
    ).reshape(1, experts_all, CAP, n_ep, part)
    moe_sum = jnp.sum(slot_weight[:, :, :, None, None] * expert_rows, axis=(1, 2))
    return (hidden_wide + moe_sum.reshape(tok_dev, model_width)).astype(BF)


def solution(mesh):
    placed = (
        P("ep", None, None, None),
        P("ctx", None),
        P("ep", None, None),
        P("ep", None),
        P(("ctx", "ep"), None, None),
        P(("ctx", "ep"), None),
        P(("ctx", "ep"), None),
        P(),
        P(),
        P(("ctx", "ep"), None),
        P(("ctx", "ep"), None),
        P("ctx", None, "ep"),
        P("ctx", None, "ep"),
        P("ctx", "ep", None),
    )
    return jax.shard_map(
        per_device, mesh=mesh, in_specs=placed, out_specs=P(("ctx", "ep"), None), check_vma=False
    )
```

```python
import functools

import jax
import jax.numpy as jnp
from jax import lax
from jax.experimental import pallas as pl
from jax.experimental.pallas import tpu as pltpu
from jax.sharding import PartitionSpec as P

BLOCK = 64
CAPB = 8
CAP = 2
FEW = 2
GROUP = 4
RING = 4
STAT_ROWS = 16
VMEM_LIMIT = 40 * 1024 * 1024
OWN_ROWS = 16

score_scale = 192.0 ** (-0.5)
masked_score = -1e30
BF = jnp.bfloat16
F32 = jnp.float32


def cut(ref, place, spans, lead=()):
    pieces = [
        ref[(*lead, pl.ds(pl.multiple_of(base + place * width, 8), width), slice(None))]
        for base, width in spans
    ]
    return jnp.concatenate(pieces, axis=0)


def split(value):
    high = value.astype(BF)
    rest = value - high.astype(F32)
    middle = rest.astype(BF)
    return high, middle, (rest - middle.astype(F32)).astype(BF)


def attend_kernel(
    count_ref, table_ref, info_ref, q_ref, prompt_ref, new_ref, *refs, spans, offset
):
    *out_refs, few, many, acc, stat = refs
    group, steps, latent, heads = q_ref.shape
    rank = out_refs[0].shape[2]
    rows = steps * heads
    first = offset + pl.program_id(0) * group
    own = info_ref[0]
    place = info_ref[1]

    def one(g, keys, n_blocks):
        sample = first + g
        count = count_ref[sample]
        for j in range(n_blocks):
            start = pl.multiple_of(table_ref[sample, j] * BLOCK, BLOCK)
            keys[j * BLOCK : (j + 1) * BLOCK, :] = prompt_ref[pl.ds(start, BLOCK), :]
        n_prompt = n_blocks * BLOCK
        keys[n_prompt : n_prompt + OWN_ROWS, :] = new_ref[g]
        n_keys = n_prompt + OWN_ROWS
        query = jnp.concatenate([q_ref[g, t] for t in range(steps)], axis=1)
        scores = jnp.dot(keys[...], query, preferred_element_type=F32) * score_scale
        key = lax.broadcasted_iota(jnp.int32, (n_keys, rows), 0)
        step = (lax.broadcasted_iota(jnp.int32, (n_keys, rows), 1) >= heads).astype(jnp.int32)
        own_last = jnp.where(own == 1, n_prompt + step, -1)
        live = (key < count * BLOCK) | ((key >= n_prompt) & (key <= own_last))
        scores = jnp.where(live, scores, masked_score)
        top = jnp.max(scores, axis=0, keepdims=True)
        weight = jnp.exp(scores - top)
        stat[g : g + 1, :rows] = top
        stat[g : g + 1, rows:] = jnp.sum(weight, axis=0, keepdims=True)
        acc[g] = lax.dot_general(
            weight.astype(BF),
            keys[:, :rank],
            (((0,), (0,)), ((), ())),
            preferred_element_type=F32,
        )
        part_rows = rows // RING
        late = (pl.program_id(0) >= pl.num_programs(0) // 2).astype(jnp.int32)
        for k, out_ref in zip((0, 2 - late, 3 - late, 1 + 2 * late), out_refs):
            part = cut(acc, lax.rem(place + k, RING), spans, (g,))
            out_ref[0, g * part_rows : (g + 1) * part_rows, :] = part.astype(BF)

    for g in range(group):
        one(g, few.at[g], FEW)
    for g in range(group):

        @pl.when(count_ref[first + g] > FEW)
        def _():
            one(g, many, CAPB)

    for i, addend in enumerate(split(stat[0:group, :])):
        stat[(i + 1) * group : (i + 2) * group, :] = addend.astype(F32)
    stat[4 * group :, :] = jnp.zeros((STAT_ROWS - 3 * group, 2 * rows), F32)
    tail = stat[group : group + STAT_ROWS, :].astype(BF)
    for out_ref in out_refs:
        out_ref[0, group * rows // RING :, :] = tail


def attend(query_t, prompt_latent, own_rows, count, table, info, rank, half, spans):
    samples, steps, latent, heads = query_t.shape
    samples = samples // 2
    rows = steps * heads
    prompt = prompt_latent.shape[0]
    groups = samples // GROUP
    skip = half * groups
    part_rows = GROUP * rows // RING + STAT_ROWS
    return pl.pallas_call(
        functools.partial(attend_kernel, spans=spans, offset=half * samples),
        grid_spec=pltpu.PrefetchScalarGridSpec(
            num_scalar_prefetch=3,
            grid=(groups,),
            in_specs=[
                pl.BlockSpec((GROUP, steps, latent, heads), lambda s, *_: (s + skip, 0, 0, 0)),
                pl.BlockSpec((prompt, latent), lambda s, *_: (0, 0)),
                pl.BlockSpec((GROUP, OWN_ROWS, latent), lambda s, *_: (s + skip, 0, 0)),
            ],
            out_specs=[pl.BlockSpec((1, part_rows, rank), lambda s, *_: (s, 0, 0))] * RING,
            scratch_shapes=[
                pltpu.VMEM((GROUP, FEW * BLOCK + OWN_ROWS, latent), BF),
                pltpu.VMEM((CAPB * BLOCK + OWN_ROWS, latent), BF),
                pltpu.VMEM((GROUP, rows, rank), F32),
                pltpu.VMEM((GROUP + STAT_ROWS, 2 * rows), F32),
            ],
        ),
        out_shape=[jax.ShapeDtypeStruct((groups, part_rows, rank), BF)] * RING,
        compiler_params=pltpu.CompilerParams(vmem_limit_bytes=VMEM_LIMIT),
        cost_estimate=pl.CostEstimate(
            flops=4 * samples * rows * FEW * BLOCK * (latent + rank),
            bytes_accessed=4 * samples * rows * (latent + rank),
            transcendentals=samples * rows * FEW * BLOCK,
        ),
    )(count, table, info, query_t, prompt_latent, own_rows)


def columns_of(stats, scratch, place, spans, total_base):
    lanes = scratch.shape[1]
    row = lax.broadcasted_iota(jnp.int32, (STAT_ROWS, lanes), 0)
    lane = lax.broadcasted_iota(jnp.int32, (STAT_ROWS, lanes), 1)
    pick = ((row % GROUP == lane) & (row < 3 * GROUP)).astype(BF)
    scratch[...] = lax.dot_general(
        stats, pick, (((0,), (0,)), ((), ())), preferred_element_type=F32
    )
    totals = [(base + total_base, width) for base, width in spans]
    return cut(scratch, place, spans), cut(scratch, place, totals)


def combined(parts, scratch, place, spans, total_base):
    body = parts[0].shape[0] - STAT_ROWS
    stats = [
        columns_of(part[body:, :], scratch.at[k], place, spans, total_base)
        for k, part in enumerate(parts)
    ]
    top = functools.reduce(jnp.maximum, [one for one, _ in stats])
    factors = [jnp.exp(one - top) for one, _ in stats]
    return top, sum(f * one for f, (_, one) in zip(factors, stats)), factors


def weighted(parts, factors, j):
    rows = factors[0].shape[0]
    return sum(
        part[j * rows : (j + 1) * rows, :].astype(F32) * factor[:, j : j + 1]
        for part, factor in zip(parts, factors)
    )


def stat_tail(scratch, addends):
    for i, addend in enumerate(addends):
        scratch[i * GROUP : (i + 1) * GROUP, :] = addend.astype(F32)
    scratch[3 * GROUP :, :] = jnp.zeros((STAT_ROWS - 3 * GROUP, scratch.shape[1]), F32)
    return scratch[...].astype(BF)


def relay_kernel(place_ref, held, ahead, behind, forward, backward, columns, lines, *, spans):
    body = held.shape[2] - STAT_ROWS
    half_width = lines.shape[2] // 2
    for side, (passed, out, k) in enumerate(((ahead, forward, 1), (behind, backward, 3))):
        parts = [held.at[side, 0], passed.at[side, 0]]
        target = lax.rem(place_ref[0] + k, RING)
        _, _, factors = combined(parts, columns, target, spans, half_width)
        for j in range(GROUP):
            rows = body // GROUP
            out[0, j * rows : (j + 1) * rows, :] = weighted(parts, factors, j).astype(BF)
        both = []
        for k, part in enumerate(parts):
            lines[k] = part[body:, :].astype(F32)
            both.append(sum(lines[k, i * GROUP : (i + 1) * GROUP, :] for i in range(3)))
        tops = [one[:, :half_width] for one in both]
        top = jnp.maximum(*tops)
        total = sum(jnp.exp(t - top) * one[:, half_width:] for t, one in zip(tops, both))
        addends = split(jnp.concatenate([top, total], axis=1))
        out[0, body:, :] = stat_tail(lines.at[0], addends)


def relay(held, ahead, behind, place, spans):
    groups, part_rows, rank = held.shape
    paired = (2, groups // 2, part_rows, rank)
    both = pl.BlockSpec((2, 1, part_rows, rank), lambda s, *_: (0, s, 0, 0))
    return pl.pallas_call(
        functools.partial(relay_kernel, spans=spans),
        grid_spec=pltpu.PrefetchScalarGridSpec(
            num_scalar_prefetch=1,
            grid=(groups // 2,),
            in_specs=[both] * 3,
            out_specs=[pl.BlockSpec((1, part_rows, rank), lambda s, *_: (s, 0, 0))] * 2,
            scratch_shapes=[
                pltpu.VMEM((2, rank, 128), F32),
                pltpu.VMEM((2, STAT_ROWS, rank), F32),
            ],
        ),
        out_shape=[jax.ShapeDtypeStruct((groups // 2, part_rows, rank), BF)] * 2,
        compiler_params=pltpu.CompilerParams(vmem_limit_bytes=VMEM_LIMIT),
        cost_estimate=pl.CostEstimate(
            flops=4 * groups * part_rows * rank,
            bytes_accessed=6 * groups * part_rows * rank,
            transcendentals=0,
        ),
    )(place, held.reshape(paired), ahead.reshape(paired), behind.reshape(paired))


def first_kernel(
    place_ref, own, ahead, behind, passed_f, passed_b, *refs, spans, next_spans
):
    *outs, columns, total, stat = refs
    rows = sum(width for _, width in spans)
    width = stat.shape[1]
    for side, parts in enumerate(
        (
            [own.at[0, 0], passed_f.at[0], behind.at[0, 0]],
            [own.at[1, 0], passed_b.at[0], ahead.at[1, 0]],
        )
    ):
        top, tot, factors = combined(parts, columns, place_ref[0], spans, width // 2)
        for j in range(GROUP):
            total[j * rows : (j + 1) * rows, :] = weighted(parts, factors, j)
        row = lax.broadcasted_iota(jnp.int32, (rows, width), 0)
        lane = lax.broadcasted_iota(jnp.int32, (rows, width), 1)
        addends = [
            sum(
                lax.dot_general(
                    value,
                    (lane == row + base).astype(BF),
                    (((0,), (0,)), ((), ())),
                    preferred_element_type=F32,
                )
                for value, base in ((one, 0), (other, rows))
            )[:GROUP, :]
            for one, other in zip(split(top), split(tot))
        ]
        tail = stat_tail(stat, addends)
        small = GROUP * rows // RING
        for k, out in enumerate(outs):
            target = lax.rem(place_ref[1] + k, RING)
            every = [(j * rows + base, w) for j in range(GROUP) for base, w in next_spans]
            out[side, 0, :small, :] = cut(total, target, every).astype(BF)
            out[side, 0, small:, :] = tail


def first_merge(own, ahead, behind, passed_f, passed_b, places, spans, next_spans):
    groups, part_rows, rank = own.shape
    rows = sum(width for _, width in spans)
    paired = (2, groups // 2, part_rows, rank)
    out_rows = GROUP * rows // RING + STAT_ROWS
    both = pl.BlockSpec((2, 1, part_rows, rank), lambda s, *_: (0, s, 0, 0))
    single = pl.BlockSpec((1, part_rows, rank), lambda s, *_: (s, 0, 0))
    outs = pl.pallas_call(
        functools.partial(first_kernel, spans=spans, next_spans=next_spans),
        grid_spec=pltpu.PrefetchScalarGridSpec(
            num_scalar_prefetch=1,
            grid=(groups // 2,),
            in_specs=[both] * 3 + [single] * 2,
            out_specs=[pl.BlockSpec((2, 1, out_rows, rank), lambda s, *_: (0, s, 0, 0))] * RING,
            scratch_shapes=[
                pltpu.VMEM((3, rank, 128), F32),
                pltpu.VMEM((GROUP * rows, rank), F32),
                pltpu.VMEM((STAT_ROWS, rank), F32),
            ],
        ),
        out_shape=[jax.ShapeDtypeStruct((2, groups // 2, out_rows, rank), BF)] * RING,
        compiler_params=pltpu.CompilerParams(vmem_limit_bytes=VMEM_LIMIT),
        cost_estimate=pl.CostEstimate(
            flops=6 * groups * part_rows * rank,
            bytes_accessed=8 * groups * part_rows * rank,
            transcendentals=0,
        ),
    )(
        places,
        own.reshape(paired),
        ahead.reshape(paired),
        behind.reshape(paired),
        passed_f,
        passed_b,
    )
    return [out.reshape(groups, out_rows, rank) for out in outs]


def last_kernel(place_ref, *refs, spans, total_base):
    *parts, out, columns = refs
    parts = [part.at[0] for part in parts]
    _, total, factors = combined(parts, columns, place_ref[0], spans, total_base)
    factors = [factor / total for factor in factors]
    rows = factors[0].shape[0]
    for j in range(GROUP):
        out[0, j * rows : (j + 1) * rows, :] = weighted(parts, factors, j).astype(BF)


def last_merge(parts, place, spans, total_base):
    groups, part_rows, rank = parts[0].shape
    out_rows = part_rows - STAT_ROWS
    return pl.pallas_call(
        functools.partial(last_kernel, spans=spans, total_base=total_base),
        grid_spec=pltpu.PrefetchScalarGridSpec(
            num_scalar_prefetch=1,
            grid=(groups,),
            in_specs=[pl.BlockSpec((1, part_rows, rank), lambda s, *_: (s, 0, 0))] * RING,
            out_specs=pl.BlockSpec((1, out_rows, rank), lambda s, *_: (s, 0, 0)),
            scratch_shapes=[pltpu.VMEM((RING, rank, 128), F32)],
        ),
        out_shape=jax.ShapeDtypeStruct((groups, out_rows, rank), BF),
        compiler_params=pltpu.CompilerParams(vmem_limit_bytes=VMEM_LIMIT),
        cost_estimate=pl.CostEstimate(
            flops=8 * groups * part_rows * rank,
            bytes_accessed=10 * groups * part_rows * rank,
            transcendentals=0,
        ),
    )(place, *parts)


def per_device(
    queries,
    prompt_latent,
    new_latent,
    blocks,
    value_up,
    w_out,
    residual,
    norm_gain,
    router,
    routes,
    bucket_slots,
    w_gate,
    w_up,
    w_down,
):
    n_ctx = lax.axis_size("ctx")
    n_ep = lax.axis_size("ep")
    devices = n_ctx * n_ep
    ctx_place = lax.axis_index("ctx")
    ep_place = lax.axis_index("ep")
    core = ep_place % 2
    swap = [(i, i ^ 1) for i in range(n_ep)]
    samples, step_count, head_count, latent = queries.shape
    rank = value_up.shape[1]
    value_width = value_up.shape[2]
    own_heads = head_count // n_ctx
    tokens_here = samples * step_count
    model_width = w_out.shape[1]
    part = model_width // n_ep

    w_rows = lax.all_gather(
        w_out,
        "ep",
        axis=0,
        axis_index_groups=[list(range(k, n_ep, 2)) for k in range(2)],
        tiled=True,
    )
    z_place, y_place = ctx_place // RING, ctx_place % RING
    ctx_axes = jnp.stack([z_place, y_place])

    inward = [(e * n_ctx + c, c * n_ep + e) for e in range(n_ep) for c in range(n_ctx)]
    outward = [(there, here) for here, there in inward]
    everywhere = ("ctx", "ep")
    choices = jnp.concatenate([routes, bucket_slots], axis=1)
    residual, choices = (lax.ppermute(value, everywhere, inward) for value in (residual, choices))
    routes, bucket_slots = jnp.split(choices, 2, axis=1)

    def along_z(k):
        return [(i, (i + k * RING) % n_ctx) for i in range(n_ctx)]

    def along_y(k):
        return [(i, i // RING * RING + (i + k) % RING) for i in range(n_ctx)]

    blk_local = prompt_latent.shape[0] // BLOCK
    shard_of = blocks // blk_local
    offset = blocks % blk_local
    is_local = (shard_of == ctx_place).astype(jnp.int32)
    position = jnp.cumsum(is_local, axis=1) - 1
    chosen = (is_local[:, :, None] == 1) & (
        position[:, :, None] == jnp.arange(CAPB)[None, None, :]
    )
    table = jnp.sum(jnp.where(chosen, offset[:, :, None], 0), axis=1)
    count = jnp.minimum(jnp.sum(is_local, axis=1), CAPB)
    own = (ctx_place == n_ctx - 1).astype(jnp.int32)
    own_rows = jnp.pad(new_latent, ((0, 0), (0, OWN_ROWS - step_count), (0, 0)))

    query_t = jnp.swapaxes(queries, 2, 3)
    per_step = head_count // RING
    by_z = [(t * head_count, per_step) for t in range(step_count)]
    by_y = [
        (t * head_count + z * per_step, own_heads) for t in range(step_count) for z in range(RING)
    ]
    second = [(t * per_step, own_heads) for t in range(step_count)]
    part_rows = step_count * per_step

    def send(forward, backward, along):
        return lax.ppermute(forward, "ctx", along(1)), lax.ppermute(backward, "ctx", along(3))

    z_first, y_first = ctx_axes, ctx_axes[::-1]
    own_a, forward_a, backward_a, held_a = attend(
        query_t, prompt_latent, own_rows, count, table, jnp.stack([own, z_place]), rank, 0, by_z
    )
    ahead_a, behind_a = send(forward_a, backward_a, along_z)
    own_b, forward_b, backward_b, held_b = attend(
        query_t, prompt_latent, own_rows, count, table, jnp.stack([own, y_place]), rank, 1, by_y
    )
    ahead_b, behind_b = send(forward_b, backward_b, along_y)
    passed_a = relay(held_a, ahead_a, behind_a, z_first, by_z)
    passed_fa, passed_ba = send(*passed_a, along_z)
    passed_b = relay(held_b, ahead_b, behind_b, y_first, by_y)
    passed_fb, passed_bb = send(*passed_b, along_y)

    value_up, _ = lax.optimization_barrier((value_up, passed_b[0]))
    own_up = lax.all_to_all(
        jnp.broadcast_to(value_up, (n_ep,) + value_up.shape[1:]),
        "ep",
        split_axis=0,
        concat_axis=0,
        tiled=True,
    )
    own_a, own_up = lax.optimization_barrier((own_a, own_up))

    next_a = first_merge(
        own_a, ahead_a, behind_a, passed_fa, passed_ba, z_first, by_z, second
    )
    next_b = first_merge(
        own_b, ahead_b, behind_b, passed_fb, passed_bb, y_first, by_y, second
    )
    got_a = [next_a[0]] + [lax.ppermute(next_a[k], "ctx", along_y(k)) for k in (1, 2, 3)]
    got_b = [next_b[0]] + [lax.ppermute(next_b[k], "ctx", along_z(k)) for k in (1, 2, 3)]
    latent_a = last_merge(got_a, y_first, second, part_rows)
    latent_b = last_merge(got_b, z_first, second, part_rows)
    latent_out = jnp.concatenate([latent_a, latent_b], axis=0)
    latent_out = latent_out.reshape(samples, step_count, own_heads, rank)
    head_values = jnp.einsum(
        "sthr,hrv->sthv", latent_out, own_up, preferred_element_type=F32
    ).astype(BF)
    head_values = head_values.reshape(tokens_here, own_heads // 2, 2, value_width)

    def pick(value, index, axis):
        return lax.dynamic_index_in_dim(value, index, axis, keepdims=False)

    kept = pick(head_values, core, 2)
    given = lax.ppermute(pick(head_values, 1 - core, 2), "ep", swap)
    head_flat = jnp.where(core == 0, jnp.stack([kept, given]), jnp.stack([given, kept]))
    theirs = jnp.dot(
        pick(head_flat, 1 - core, 0).reshape(tokens_here, -1), w_rows, preferred_element_type=F32
    ).astype(BF)
    theirs = lax.ppermute(theirs, "ep", swap)
    ours = jnp.dot(
        pick(head_flat, core, 0).reshape(tokens_here, -1), w_rows, preferred_element_type=F32
    )
    projected = (ours + theirs.astype(F32)).astype(BF)
    tok_dev = residual.shape[0]
    projected = lax.all_to_all(
        projected.reshape(n_ctx, tok_dev, model_width),
        "ctx",
        split_axis=0,
        concat_axis=0,
        tiled=True,
    )
    attention = jnp.sum(projected.astype(F32), axis=0)

    hidden_state = (residual.astype(F32) + attention).astype(BF)
    hidden_wide = hidden_state.astype(F32)
    mean_square = jnp.mean(hidden_wide * hidden_wide, axis=1, keepdims=True)
    normed = (hidden_wide * lax.rsqrt(mean_square + 1e-06) * norm_gain).astype(BF)
    affinity = jax.nn.sigmoid(jnp.dot(normed, router, preferred_element_type=F32))
    experts_all = router.shape[1]
    experts = jnp.arange(experts_all)
    picked = (routes[:, :, None] == experts[None, None, :]).astype(F32)
    picked_aff = jnp.sum(picked * affinity[:, None, :], axis=2)
    combine_w = 2.5 * picked_aff / jnp.sum(picked_aff, axis=1, keepdims=True)
    kept_route = bucket_slots < CAP
    hits = picked[:, :, :, None] * (
        (bucket_slots[:, :, None] == jnp.arange(CAP)[None, None, :]) & kept_route[:, :, None]
    ).astype(F32)[:, :, None, :]
    slot_hit = jnp.sum(hits, axis=1).reshape(tok_dev, experts_all * CAP)
    slot_weight = jnp.sum(hits * combine_w[:, :, None, None], axis=1)
    slot_weight = lax.ppermute(
        slot_weight.reshape(tok_dev, experts_all * CAP), everywhere, outward
    ).reshape(tok_dev, experts_all, CAP)
    hidden_wide = lax.ppermute(hidden_state, everywhere, outward).astype(F32)

    outgoing = jnp.einsum(
        "te,td->ed", slot_hit.astype(BF), normed, preferred_element_type=F32
    ).astype(BF)
    chips = n_ep // CAP
    copies = jnp.broadcast_to(
        outgoing.reshape(n_ctx, 1, CAP, n_ep, part), (n_ctx, chips, CAP, n_ep, part)
    ).reshape(devices, n_ep, part)
    arrived = lax.all_to_all(copies, ("ctx", "ep"), split_axis=0, concat_axis=0, tiled=True)
    arrived = arrived.reshape(devices, model_width)
    sibling = lax.ppermute(arrived, "ep", swap)
    rows = jnp.concatenate([arrived, sibling], axis=0)
    gate_act = jnp.dot(rows, w_gate[0], preferred_element_type=F32)
    up_act = jnp.dot(rows, w_up[0], preferred_element_type=F32)
    inner_act = (jax.nn.silu(gate_act) * up_act).astype(BF)
    theirs = jnp.dot(inner_act[devices:], w_down[0], preferred_element_type=F32).astype(BF)
    theirs = lax.ppermute(theirs, "ep", swap)
    ours = jnp.dot(inner_act[:devices], w_down[0], preferred_element_type=F32)
    pair_out = (ours + theirs.astype(F32)).astype(BF).reshape(n_ctx, n_ep, n_ep, part)
    pair_out = pair_out.swapaxes(0, 1).reshape(devices, n_ep, part)
    returned = lax.all_to_all(pair_out, ("ctx", "ep"), split_axis=0, concat_axis=0, tiled=True)
    expert_rows = jnp.sum(
        returned.reshape(n_ctx, chips, CAP, n_ep, part).astype(F32), axis=1
    ).reshape(1, experts_all, CAP, n_ep, part)
    moe_sum = jnp.sum(slot_weight[:, :, :, None, None] * expert_rows, axis=(1, 2))
    return (hidden_wide + moe_sum.reshape(tok_dev, model_width)).astype(BF)


def solution(mesh):
    placed = (
        P("ep", None, None, None),
        P("ctx", None),
        P("ep", None, None),
        P("ep", None),
        P(("ctx", "ep"), None, None),
        P(("ctx", "ep"), None),
        P(("ctx", "ep"), None),
        P(),
        P(),
        P(("ctx", "ep"), None),
        P(("ctx", "ep"), None),
        P("ctx", None, "ep"),
        P("ctx", None, "ep"),
        P("ctx", "ep", None),
    )
    return jax.shard_map(
        per_device, mesh=mesh, in_specs=placed, out_specs=P(("ctx", "ep"), None), check_vma=False
    )
```
